32 devices in a mesh: batch: 4 (over y, core), seq: 8 (over z, x).
Axes of the slice: x: 2, y: 2, z: 4, core: 2. Of those that a mesh axis runs over, the one named last changes fastest.
Arguments:
- tokens: bfloat16 [4, 2560, 2048], P('batch', 'seq'), may hold values from -6 to 6
- doc_lengths: int32 [4, 3], P('batch'), may hold values from 1 to 2558, as said below
- out_grad: bfloat16 [4, 2560, 2048], P('batch', 'seq'), may hold values from -6 to 6
- mix_gain: bfloat16 [2048], P(('batch', 'seq')), may hold values from 0.25 to 1.75
- branch_weight: bfloat16 [2048, 2560], P(('batch', 'seq')), may hold values from -0.125 to 0.125
- input_weight: bfloat16 [2048, 2560], P(('batch', 'seq')), may hold values from -0.125 to 0.125
- branch_bias: bfloat16 [2560], P(('batch', 'seq')), may hold values from -3 to 3
- input_bias: bfloat16 [2560], P(('batch', 'seq')), may hold values from -3 to 3
- conv_taps: bfloat16 [2560, 4], P(('batch', 'seq')), may hold values from -3 to 3
- conv_bias: bfloat16 [2560], P(('batch', 'seq')), may hold values from -3 to 3
- rate_weight: bfloat16 [2560, 160], P(('batch', 'seq')), may hold values from -0.5 to 0.5
- entry_weight: bfloat16 [2560, 160], P(('batch', 'seq')), may hold values from -0.5 to 0.5
- rate_bias: bfloat16 [2560], P(('batch', 'seq')), may hold values from -4 to 4
- entry_bias: bfloat16 [2560], P(('batch', 'seq')), may hold values from -4 to 4
- decay_param: bfloat16 [2560], P(('batch', 'seq')), may hold values from 3 to 16
- out_weight: bfloat16 [2048, 2560], P(('batch', 'seq')), may hold values from -0.5 to 0.5
- out_bias: bfloat16 [2048], P(('batch', 'seq')), may hold values from -2 to 2
- mlp_gain: bfloat16 [2048], P(('batch', 'seq')), may hold values from 0.25 to 1.75
- gate_weight: bfloat16 [2048, 6144], P(('batch', 'seq')), may hold values from -0.125 to 0.125
- up_weight: bfloat16 [2048, 6144], P(('batch', 'seq')), may hold values from -0.125 to 0.125
- down_weight: bfloat16 [2048, 6144], P(('batch', 'seq')), may hold values from -0.15625 to 0.15625
Outputs:
- block_out: bfloat16 [4, 2560, 2048], P('batch', 'seq')
- tokens_grad: float32 [4, 2560, 2048], P('batch', 'seq')
- mix_gain_grad: float32 [2048], P(('batch', 'seq'))
- branch_weight_grad: float32 [2048, 2560], P(('batch', 'seq'))
- input_weight_grad: float32 [2048, 2560], P(('batch', 'seq'))
- branch_bias_grad: float32 [2560], P(('batch', 'seq'))
- input_bias_grad: float32 [2560], P(('batch', 'seq'))
- conv_taps_grad: float32 [2560, 4], P(('batch', 'seq'))
- conv_bias_grad: float32 [2560], P(('batch', 'seq'))
- rate_weight_grad: float32 [2560, 160], P(('batch', 'seq'))
- entry_weight_grad: float32 [2560, 160], P(('batch', 'seq'))
- rate_bias_grad: float32 [2560], P(('batch', 'seq'))
- entry_bias_grad: float32 [2560], P(('batch', 'seq'))
- decay_param_grad: float32 [2560], P(('batch', 'seq'))
- out_weight_grad: float32 [2048, 2560], P(('batch', 'seq'))
- out_bias_grad: float32 [2048], P(('batch', 'seq'))
- mlp_gain_grad: float32 [2048], P(('batch', 'seq'))
- gate_weight_grad: float32 [2048, 6144], P(('batch', 'seq'))
- up_weight_grad: float32 [2048, 6144], P(('batch', 'seq'))
- down_weight_grad: float32 [2048, 6144], P(('batch', 'seq'))
The draws below stay inside these ranges and needn't reach their ends.
Inputs may be any that keep to these rules, and one draw needn't show every extreme that they name: `doc_lengths`: each group has three documents whose lengths sum to 2560; the first and the last have 1 to 320 tokens each, the middle one the rest.
All inputs are finite; a program needn't handle non-finite values.
Results may differ from the reference program's by a relative error of at most 0.0092.
Values may be sent and summed in bfloat16 or wider, within the bound.
No kernel may reach another device: no remote copies, remote signals or barrier semaphores. Data moves between devices by JAX's collectives and lax.ppermute only.
A program may use at most 512 MiB of HBM per device.

```python
import math
import jax
import jax.numpy as jnp
from jax import lax

D = 2048
R = 2560
F = 6144
CONV = 4
TOK_DEV = 320
BW = 160
GROUP_TOK = 2560
GROUPS = 4


def draw_doc_lengths(key, part):
    key = jax.random.fold_in(key, 23)
    head_key, tail_key = jax.random.split(key)
    first_len = jax.random.randint(head_key, (GROUPS, 1), 1, TOK_DEV // 2 + 1)
    last_len = jax.random.randint(tail_key, (GROUPS, 1), 1, TOK_DEV // 2 + 1)
    middle_len = GROUP_TOK - first_len - last_len
    return jnp.concatenate([first_len, middle_len, last_len], axis=1).astype(jnp.int32)


def draw_decay_param(key, part):
    key = jax.random.fold_in(key, 11)
    pick_key, slow_key, fast_key = jax.random.split(key, 3)
    slow_share = 0.5
    pick = jax.random.uniform(pick_key, (R,), jnp.float32)
    slow_rate = jnp.exp(jax.random.uniform(slow_key, (R,), jnp.float32, math.log(0.02 / GROUP_TOK), math.log(0.25 / GROUP_TOK)))
    fast_rate = jnp.exp(jax.random.uniform(fast_key, (R,), jnp.float32, math.log(0.008), math.log(0.03)))
    rate_val = jnp.where(pick < slow_share, slow_rate, fast_rate)
    return (-jnp.log(jnp.expm1(rate_val))).astype(jnp.bfloat16)


def block_levels(own_key, shape, cuts, least, high):
    loudness, own = 1.0, jax.random.fold_in(own_key, 6)
    for position, parts in cuts:
        steps = jnp.exp(jax.random.uniform(jax.random.fold_in(own, position), (parts,), jnp.float32, least / len(cuts), high / len(cuts)))
        loudness = loudness * jnp.repeat(steps, shape[position] // parts).reshape([-1 if axis == position else 1 for axis in range(len(shape))])
    return loudness


def scatter_about(key, shape, width, bound, pieces=(), kind=jnp.bfloat16):
    factor_of = block_levels(key, shape, pieces, -0.22, 0.18) if pieces else 1.0
    values = jax.random.normal(key, shape, jnp.float32) * width * factor_of
    return jnp.minimum(jnp.maximum(values, -bound), bound).astype(kind)


def setup_inputs(seed: int = 0) -> dict:
    keys = jax.random.split(jax.random.key(seed), 22)
    tokens = scatter_about(keys[0], (GROUPS, GROUP_TOK, D), 1.0, 6.0, ((0, 4), (1, 8)))
    doc_lengths = draw_doc_lengths(jax.random.fold_in(keys[21], 71), 0)
    out_grad = scatter_about(keys[2], (GROUPS, GROUP_TOK, D), 1.0, 6.0, ((0, 4), (1, 8)))
    mix_gain = jnp.clip(1.0 + 0.15 * jax.random.normal(keys[3], (D,), jnp.float32), 0.25, 1.75).astype(jnp.bfloat16)
    branch_weight = scatter_about(keys[4], (D, R), D ** -0.5, 0.125, ((0, 32),))
    input_weight = scatter_about(keys[5], (D, R), D ** -0.5, 0.125, ((0, 32),))
    branch_bias = scatter_about(keys[6], (R,), 0.5, 3.0, ((0, 32),))
    input_bias = scatter_about(keys[7], (R,), 0.5, 3.0, ((0, 32),))
    conv_taps = scatter_about(keys[8], (R, CONV), CONV ** -0.5, 3.0, ((0, 32),))
    conv_bias = scatter_about(keys[9], (R,), 0.5, 3.0, ((0, 32),))
    rate_weight = scatter_about(keys[10], (R, BW), BW ** -0.5, 0.5, ((0, 32),))
    entry_weight = scatter_about(keys[11], (R, BW), BW ** -0.5, 0.5, ((0, 32),))
    rate_bias = scatter_about(keys[12], (R,), 1.0, 4.0, ((0, 32),))
    entry_bias = scatter_about(keys[13], (R,), 1.0, 4.0, ((0, 32),))
    decay_param = draw_decay_param(jax.random.fold_in(keys[21], 71), 0)
    out_weight = scatter_about(keys[15], (D, R), (R // 16) ** -0.5, 0.5, ((0, 32),))
    out_bias = scatter_about(keys[16], (D,), 0.3, 2.0, ((0, 32),))
    mlp_gain = jnp.clip(1.0 + 0.15 * jax.random.normal(keys[17], (D,), jnp.float32), 0.25, 1.75).astype(jnp.bfloat16)
    gate_weight = scatter_about(keys[18], (D, F), D ** -0.5, 0.125, ((0, 32),))
    up_weight = scatter_about(keys[19], (D, F), D ** -0.5, 0.125, ((0, 32),))
    down_weight = scatter_about(keys[20], (D, F), (F // 4) ** -0.5, 0.15625, ((0, 32),))
    return {"tokens": tokens, "doc_lengths": doc_lengths, "out_grad": out_grad, "mix_gain": mix_gain, "branch_weight": branch_weight, "input_weight": input_weight, "branch_bias": branch_bias, "input_bias": input_bias, "conv_taps": conv_taps, "conv_bias": conv_bias, "rate_weight": rate_weight, "entry_weight": entry_weight, "rate_bias": rate_bias, "entry_bias": entry_bias, "decay_param": decay_param, "out_weight": out_weight, "out_bias": out_bias, "mlp_gain": mlp_gain, "gate_weight": gate_weight, "up_weight": up_weight, "down_weight": down_weight}


HIGH = lax.Precision.HIGHEST

@jax.custom_vjp
def low(v):
    return lax.optimization_barrier(v.astype(jnp.bfloat16)).astype(jnp.float32)

@jax.custom_vjp
def low_back(v):
    return v

def low_keep(v):
    return (low(v), None)

def low_pass(kept, grad):
    return (grad,)

def back_keep(v):
    return (v, None)

def back_low(kept, grad):
    return (low(grad),)
low.defvjp(low_keep, low_pass)
low_back.defvjp(back_keep, back_low)

def gelu_tanh(values):
    return jax.nn.gelu(values, approximate=True)

def rms_scale(values, gain_vec):
    return values * lax.rsqrt(lax.optimization_barrier(jnp.mean(values * values, axis=-1, keepdims=True)) + 1e-06) * gain_vec

def compose(earlier, later):
    return (earlier[0] * later[0], later[0] * earlier[1] + later[1])

def doc_layout(lengths_row, first_pos, span_count):
    doc_ends = jnp.cumsum(lengths_row).astype(jnp.int32)
    doc_starts = jnp.concatenate([jnp.zeros((1,), jnp.int32), doc_ends[:-1]], axis=0)
    places = (first_pos + jnp.arange(span_count, dtype=jnp.int32)).astype(jnp.int32)
    start_mask = jnp.any(places[:, None] == doc_starts[None, :], axis=1)
    begins = lax.optimization_barrier(jnp.max(jnp.where(doc_starts[None, :] <= places[:, None], doc_starts[None, :], 0), axis=1)).astype(jnp.int32)
    return (places, start_mask, begins)

def lru_gates(rate_in, entry_in, conv_in, decay_in, keep_mask, start_mask):
    rate_sig = jax.nn.sigmoid(rate_in)
    entry_sig = jax.nn.sigmoid(entry_in)
    log_decay = -8.0 * rate_sig * jax.nn.softplus(-decay_in)
    drive_scale = jnp.where(start_mask[:, None], 1.0, jnp.sqrt(-jnp.expm1(2.0 * log_decay)))
    return (jnp.exp(log_decay) * keep_mask[:, None], drive_scale * entry_sig * conv_in)

def hawk_block(group_in, lengths_row, mix_gain, branch_weight, input_weight, branch_bias, input_bias, conv_taps, conv_bias, rate_weight, entry_weight, rate_bias, entry_bias, decay_param, out_weight, out_bias, mlp_gain, gate_weight, up_weight, down_weight):
    tok_rows = group_in.shape[0]
    width_r = branch_weight.shape[1]
    block_w = rate_weight.shape[1]
    head_count = width_r // block_w
    tap_count = conv_taps.shape[1]
    places, start_mask, begins = doc_layout(lengths_row, 0, tok_rows)
    keep_mask = 1.0 - start_mask.astype(jnp.float32)
    normed = low(rms_scale(group_in, mix_gain))
    branch_val = gelu_tanh(low_back(jnp.dot(normed, branch_weight, precision=HIGH) + branch_bias))
    conv_in = low(low_back(jnp.dot(normed, input_weight, precision=HIGH) + input_bias))
    padded = jnp.concatenate([jnp.zeros((tap_count - 1, width_r), jnp.float32), conv_in], axis=0)
    conv_val = jnp.zeros((tok_rows, width_r), jnp.float32) + conv_bias
    for offset in range(tap_count):
        valid_mask = (places - offset >= begins).astype(jnp.float32)[:, None]
        conv_val = conv_val + conv_taps[:, offset] * padded[tap_count - 1 - offset:tap_count - 1 - offset + tok_rows] * valid_mask
    conv_out = low(low_back(conv_val))
    grouped = conv_out.reshape(tok_rows, head_count, block_w)
    rate_pre = low_back(jnp.einsum('thj,hjk->thk', grouped, rate_weight.reshape(head_count, block_w, block_w), precision=HIGH).reshape(tok_rows, width_r) + rate_bias)
    entry_pre = low_back(jnp.einsum('thj,hjk->thk', grouped, entry_weight.reshape(head_count, block_w, block_w), precision=HIGH).reshape(tok_rows, width_r) + entry_bias)
    decay_a, drive = lru_gates(rate_pre, entry_pre, conv_out, decay_param, keep_mask, start_mask)
    cum_decay, hidden = lax.associative_scan(compose, (decay_a, drive))
    merged = low(hidden * branch_val)
    residual = group_in + low_back(jnp.dot(merged, out_weight.T, precision=HIGH) + out_bias)
    normed_two = low(rms_scale(residual, mlp_gain))
    gate_pre = low_back(jnp.dot(normed_two, gate_weight, precision=HIGH))
    up_pre = low_back(jnp.dot(normed_two, up_weight, precision=HIGH))
    activated = low(gelu_tanh(gate_pre) * up_pre)
    return residual + low_back(jnp.dot(activated, down_weight.T, precision=HIGH))

def reference(tokens, doc_lengths, out_grad, mix_gain, branch_weight, input_weight, branch_bias, input_bias, conv_taps, conv_bias, rate_weight, entry_weight, rate_bias, entry_bias, decay_param, out_weight, out_bias, mlp_gain, gate_weight, up_weight, down_weight):
    params = tuple((weight_in.astype(jnp.float32) for weight_in in (mix_gain, branch_weight, input_weight, branch_bias, input_bias, conv_taps, conv_bias, rate_weight, entry_weight, rate_bias, entry_bias, decay_param, out_weight, out_bias, mlp_gain, gate_weight, up_weight, down_weight)))

    def group_step(totals, group_item):
        group_x, lengths_row, group_grad = group_item

        def run_block(group_in, *weights_in):
            return hawk_block(group_in, lengths_row, *weights_in)
        result, pull_back = jax.vjp(run_block, group_x, *params)
        gradients = pull_back(group_grad)
        totals = tuple((total + part for total, part in zip(totals, gradients[1:])))
        return (totals, (result, gradients[0]))
    start_totals = tuple((jnp.zeros(param.shape, jnp.float32) for param in params))
    totals, (outputs, input_grads) = lax.scan(group_step, start_totals, (tokens.astype(jnp.float32), doc_lengths, out_grad.astype(jnp.float32)))
    return (outputs.astype(jnp.bfloat16), input_grads, totals[0], totals[1], totals[2], totals[3], totals[4], totals[5], totals[6], totals[7], totals[8], totals[9], totals[10], totals[11], totals[12], totals[13], totals[14], totals[15], totals[16], totals[17])
```

```python
import functools

import jax
import jax.numpy as jnp
from jax import lax
from jax.experimental import pallas as pl
from jax.experimental.pallas import tpu as pltpu
from jax.sharding import PartitionSpec as P

RIM = 16


def plain_dot(first_op, second_op):
    return jnp.dot(first_op, second_op, preferred_element_type=jnp.float32)


def outer_sum(first_op, second_op):
    return lax.dot_general(
        first_op, second_op, (((0,), (0,)), ((), ())), preferred_element_type=jnp.float32
    )


def against_rows(first_op, second_op):
    return lax.dot_general(
        first_op, second_op, (((1,), (1,)), ((), ())), preferred_element_type=jnp.float32
    )


def gelu_tanh(values):
    return jax.nn.gelu(values, approximate=True)


def low(values):
    return values.astype(jnp.bfloat16)


def wide(values):
    return values.astype(jnp.float32)


def across_batch(block, flip):
    count = lax.axis_size("batch")
    return lax.ppermute(block, "batch", [(i, i ^ flip) for i in range(count)])


def gather_batch(block):
    over = across_batch(block, 2)
    return [block, across_batch(block, 1), over, across_batch(over, 1)]


def scatter_batch(parts):
    mine = wide(parts[0]) + wide(across_batch(parts[1], 1))
    over = wide(parts[2]) + wide(across_batch(parts[3], 1))
    return mine + wide(across_batch(low(over), 2))


def flip_x(block):
    return lax.ppermute(block, "seq", [(i, i ^ 1) for i in range(lax.axis_size("seq"))])


def along_z(block, hops):
    return lax.ppermute(block, "seq", [(2 * a + x, 2 * b + x) for a, b in hops for x in range(2)])


def flip_z(block, by):
    return along_z(block, [(i, i ^ by) for i in range(lax.axis_size("seq") // 2)])


def after(value, *others):
    return lax.optimization_barrier((value, *others))[0]


def gather_z(block):
    count = lax.axis_size("seq") // 2
    if count != 4:
        return [block] + [flip_z(block, k) for k in range(1, count)]
    near = flip_z(block, 1)
    far = flip_z(block, 2)
    mid = along_z(block, [(1, 2), (2, 1)])
    end = along_z(far, [(1, 0), (2, 3)])
    z = lax.axis_index("seq") // 2
    return [block, near, far, jnp.where(jnp.logical_or(z == 1, z == 2), mid, end)]


def gather_seq(block, cuts):
    blocks = gather_z(block)
    other = []
    for first, last in zip(cuts[:-1], cuts[1:]):
        group = blocks[first:last]
        other.append(flip_x(group[0] if len(group) == 1 else jnp.concatenate(group, axis=0)))
    return jnp.concatenate(blocks + other, axis=0)


def scatter_seq(term, send_type):
    count = lax.axis_size("seq") // 2
    half = term.shape[0] // 2
    rows = half // count
    got = flip_x(term[half:].astype(send_type))

    def column(k):
        at = slice(k * rows, (k + 1) * rows)
        return wide(term[at]) + wide(got[at])

    if count != 4:
        total = column(0)
        for k in range(1, count):
            total = total + wide(flip_z(column(k).astype(send_type), k))
        return total
    third = column(3).astype(send_type)
    from_end = along_z(third, [(0, 1), (3, 2)])
    from_mid = along_z(third, [(1, 2), (2, 1)])
    from_far = flip_z((column(2) + wide(from_end)).astype(send_type), 2)
    from_near = flip_z(column(1).astype(send_type), 1)
    return column(0) + wide(from_near) + wide(from_far) + wide(from_mid)


def by_place(parts):
    b = lax.axis_index("batch")
    out = []
    for j in range(4):
        pick = parts[j]
        for place in range(1, 4):
            pick = jnp.where(b == place, parts[j ^ place], pick)
        out.append(pick)
    return out


def split_columns(weights, common=None):
    b = lax.axis_index("batch")
    parts = []
    for k in range(4):
        part = []
        for weight in weights:
            width = weight.shape[1] // 4
            part.append(lax.dynamic_slice_in_dim(weight, (b ^ k) * width, width, 1))
        if common is not None:
            part.append(common)
        part = part[0] if len(part) == 1 else jnp.concatenate(part, axis=1)
        parts.append(part if k == 0 else across_batch(part, k))
    return jnp.concatenate(by_place(parts), axis=0)


def join_columns(share):
    b = lax.axis_index("batch")
    rows = share.shape[0] // 4
    got = []
    for k in range(4):
        part = low(lax.dynamic_slice_in_dim(share, (b ^ k) * rows, rows, 0))
        got.append(part if k == 0 else across_batch(part, k))
    return got


def whole_rows(parts):
    return jnp.concatenate([wide(p) for p in by_place(parts)], axis=1)


def carried_in(part, reverse):
    s = lax.axis_index("seq")
    count = lax.axis_size("seq")
    total_a, total_b = part[0], part[1]
    enter_a, enter_b = jnp.ones_like(total_a), jnp.zeros_like(total_b)
    bit = 1
    while bit < count:
        both = jnp.stack([total_a, total_b])
        got = lax.ppermute(both, "seq", [(i, i ^ bit) for i in range(count)])
        got_a, got_b = got[0], got[1]
        theirs_first = ((s & bit) == 0) if reverse else ((s & bit) != 0)
        enter_b = jnp.where(theirs_first, enter_a * got_b + enter_b, enter_b)
        enter_a = jnp.where(theirs_first, enter_a * got_a, enter_a)
        total_b = jnp.where(theirs_first, total_a * got_b + total_b, got_a * total_b + got_b)
        total_a = total_a * got_a
        bit *= 2
    return enter_b


def scan_kernel(reverse, a_ref, b_ref, cum_ref, out_ref):
    groups, rows, lanes = a_ref.shape
    tiles = rows // 8
    row = lax.broadcasted_iota(jnp.int32, (8, lanes), 0)

    def step(i, carry):
        tile = tiles - 1 - i if reverse else i
        at = pl.ds(pl.multiple_of(tile * 8, 8), 8)
        after = []
        for g in range(groups):
            a, b = a_ref[g, at, :], b_ref[g, at, :]
            for shift in (1, 2, 4):
                by = 8 - shift if reverse else shift
                ok = row < 8 - shift if reverse else row >= shift
                a_far = jnp.where(ok, pltpu.roll(a, by, 0), 1.0)
                b_far = jnp.where(ok, pltpu.roll(b, by, 0), 0.0)
                b = b + a * b_far
                a = a * a_far
            cum, state = carry[g]
            b = b + a * state
            a = a * cum
            cum_ref[g, at, :] = a
            out_ref[g, at, :] = b
            last = 0 if reverse else 7
            after.append(
                (
                    jnp.broadcast_to(a[last : last + 1], (8, lanes)),
                    jnp.broadcast_to(b[last : last + 1], (8, lanes)),
                )
            )
        return tuple(after)

    start = tuple(
        (jnp.ones((8, lanes), jnp.float32), jnp.zeros((8, lanes), jnp.float32))
        for _ in range(groups)
    )
    lax.fori_loop(0, tiles, step, start)


def local_scan(decay, drive, reverse):
    groups, rows, width = decay.shape
    lanes = 128
    spec = pl.BlockSpec((groups, rows, lanes), lambda i: (0, 0, i))
    shape = jax.ShapeDtypeStruct(decay.shape, jnp.float32)
    return pl.pallas_call(
        functools.partial(scan_kernel, reverse),
        grid=(width // lanes,),
        in_specs=[spec, spec],
        out_specs=[spec, spec],
        out_shape=[shape, shape],
        cost_estimate=pl.CostEstimate(
            flops=20 * decay.size, bytes_accessed=16 * decay.size, transcendentals=0
        ),
    )(decay, drive)


def doc_layout(lengths, first_pos, span_count):
    doc_ends = jnp.cumsum(lengths, axis=1)
    doc_starts = jnp.concatenate([jnp.zeros_like(doc_ends[:, :1]), doc_ends[:, :-1]], axis=1)
    places = first_pos + jnp.arange(span_count, dtype=jnp.int32)
    at_start = places[None, :, None] == doc_starts[:, None, :]
    before = doc_starts[:, None, :] <= places[None, :, None]
    begins = jnp.max(jnp.where(before, doc_starts[:, None, :], 0), axis=2)
    return places, jnp.any(at_start, axis=2), begins


def lru_gates(rate_in, entry_in, conv_in, decay_in, keep_mask, start_mask):
    rate_sig = jax.nn.sigmoid(rate_in)
    entry_sig = jax.nn.sigmoid(entry_in)
    log_decay = -8.0 * rate_sig * jax.nn.softplus(-decay_in)
    drive_scale = jnp.where(start_mask, 1.0, jnp.sqrt(-jnp.expm1(2.0 * log_decay)))
    return (jnp.exp(log_decay) * keep_mask, drive_scale * entry_sig * conv_in)


def inv_root(values):
    return lax.rsqrt(jnp.mean(values * values, axis=-1, keepdims=True) + 1e-06)


def norm_backward(values, scale, gain_vec, incoming):
    weighted = incoming * gain_vec
    inner_mean = jnp.mean(weighted * values, axis=-1, keepdims=True)
    return (
        scale * weighted - values * scale * scale * scale * inner_mean,
        jnp.sum(incoming * values * scale, axis=0),
    )


def head_diagonal(blocks, heads, width):
    size = heads * width
    own = lax.broadcasted_iota(jnp.int32, (size, size), 0) // width
    at = lax.broadcasted_iota(jnp.int32, (size, size), 1) // width
    return jnp.where(own == at, jnp.tile(blocks, (1, heads)), jnp.zeros((), blocks.dtype))


def head_blocks(dense, heads, width):
    return jnp.concatenate(
        [dense[h * width : (h + 1) * width, h * width : (h + 1) * width] for h in range(heads)], 0
    )


def order_matrix(seq, own_d):
    s = lax.axis_index("seq")
    size = 4 * seq * own_d
    d = lax.broadcasted_iota(jnp.int32, (size, size), 0)
    at = lax.broadcasted_iota(jnp.int32, (size, size), 1)
    place_b, rest = d // (seq * own_d), d % (seq * own_d)
    away = (rest // own_d) ^ s
    row = (((away % 2) * (seq // 2) + away // 2) * 4 + place_b) * own_d + rest % own_d
    return (row == at).astype(jnp.bfloat16)


def channel_matrix(seq, own_r):
    s = lax.axis_index("seq")
    size = seq * own_r
    r = lax.broadcasted_iota(jnp.int32, (size, size), 0)
    at = lax.broadcasted_iota(jnp.int32, (size, size), 1)
    away = (at // own_r) ^ s
    row = ((away % 2) * (seq // 2) + away // 2) * own_r + at % own_r
    return (row == r).astype(jnp.bfloat16)


def reorder(values, matrix, back=False):
    dot = against_rows if back else plain_dot
    if values.dtype == jnp.bfloat16:
        return low(dot(values, matrix))
    first = low(values)
    rest = values - wide(first)
    second = low(rest)
    third = low(rest - wide(second))
    return dot(first, matrix) + dot(second, matrix) + dot(third, matrix)


def shards(
    tokens,
    doc_lengths,
    out_grad,
    mix_gain,
    branch_weight,
    input_weight,
    branch_bias,
    input_bias,
    conv_taps,
    conv_bias,
    rate_weight,
    entry_weight,
    rate_bias,
    entry_bias,
    decay_param,
    out_weight,
    out_bias,
    mlp_gain,
    gate_weight,
    up_weight,
    down_weight,
):
    seq = lax.axis_size("seq")
    rows, model = tokens.shape[1:]
    block_w = rate_weight.shape[1]
    tap_count = conv_taps.shape[1]
    width = branch_weight.shape[1] // 4
    hidden_w = gate_weight.shape[1] // 4
    heads = width // block_w
    own_r = conv_bias.shape[0]
    own_d = mix_gain.shape[0]
    groups = 4
    single = tuple(range(seq // 2 + 1))
    halves = (0, seq // 4, seq // 2)

    order = order_matrix(seq, own_d)
    model_vec = jnp.stack([mix_gain, mlp_gain, out_bias], axis=1)
    model_vec = jnp.pad(model_vec, ((0, 0), (0, 125)))
    input_rows = split_columns([input_weight], model_vec)
    rim = lax.ppermute(tokens[0, rows - RIM :], "seq", [(i, i + 1) for i in range(seq - 1)])
    own_extended = reorder(jnp.concatenate([rim, tokens[0]], axis=0), order)
    own_tokens = own_extended[RIM:]
    input_all = gather_seq(input_rows, single)
    extended_parts = gather_batch(after(own_extended, input_rows))
    branch_rows, out_rows = jnp.split(
        split_columns([after(branch_weight, input_rows), out_weight]), [width], axis=1
    )
    branch_full = gather_seq(branch_rows, single)
    out_full = gather_seq(after(out_rows, branch_full), single)
    mlp_rows = split_columns([after(gate_weight, extended_parts[2], out_rows), up_weight, down_weight])
    two_rows, down_rows = jnp.split(after(mlp_rows, out_full), [2 * hidden_w], axis=1)
    two_full = gather_seq(two_rows, halves)
    down_full = gather_seq(after(down_rows, two_full), halves)
    grad_low = reorder(out_grad[0], order)
    grad_all = jnp.concatenate(gather_batch(after(grad_low, mlp_rows)), axis=0)

    vectors = jnp.stack(
        [branch_bias, input_bias, conv_bias, rate_bias, entry_bias, decay_param], axis=1
    )
    lane_pad = -(2 * block_w + tap_count + 6) % 128
    pack = jnp.concatenate(
        [rate_weight, entry_weight, conv_taps, vectors, jnp.zeros((own_r, lane_pad), jnp.bfloat16)],
        axis=1,
    )
    channels = channel_matrix(seq, own_r)
    by_channel = low(
        outer_sum(channels, gather_seq(after(pack, input_rows), (0, seq // 2)))
    )
    rate_dense = head_diagonal(by_channel[:, :block_w], heads, block_w)
    entry_dense = head_diagonal(by_channel[:, block_w : 2 * block_w], heads, block_w)
    channel_vec = wide(by_channel[:, 2 * block_w : 2 * block_w + tap_count + 6]).T
    tap_vals = channel_vec[:tap_count]
    branch_b, input_b, conv_b, rate_b, entry_b, decay_full = [
        channel_vec[tap_count + i] for i in range(6)
    ]

    lengths = jnp.concatenate([doc_lengths] + [across_batch(doc_lengths, k) for k in (1, 2, 3)], 0)
    start_pos = lax.axis_index("seq") * rows
    places, start_mask, begins = doc_layout(lengths, start_pos, rows + tap_count - 1)
    own_start = start_mask[:, :rows, None]
    keep_mask = 1.0 - own_start.astype(jnp.float32)

    input_full = input_all[:, :width]
    model_full = wide(input_all[:, width : width + 3]).T
    mix_scale, mlp_scale, out_b = model_full[0], model_full[1], model_full[2]
    extended = jnp.stack(extended_parts)
    inputs_all = wide(extended)
    scale_all = inv_root(inputs_all)
    normed_ext = low(inputs_all * scale_all * mix_scale)
    normed_low = normed_ext[:, RIM:].reshape(groups * rows, model)
    conv_in = low(plain_dot(normed_ext.reshape(-1, model), input_full) + input_b).reshape(
        groups, rows + RIM, width
    )

    def behind(offset):
        return conv_in[:, RIM - offset : RIM - offset + rows]

    def valid(offset, ahead):
        at = slice(offset, offset + rows) if ahead else slice(0, rows)
        return wide(places[at] - offset >= begins[:, at])[:, :, None]

    conv_val = jnp.zeros((groups, rows, width), jnp.float32) + conv_b
    for offset in range(tap_count):
        conv_val = conv_val + tap_vals[offset] * wide(behind(offset)) * valid(offset, False)
    conv_low = low(conv_val)
    conv_flat = conv_low.reshape(groups * rows, width)
    rate_pre = (plain_dot(conv_flat, rate_dense) + rate_b).reshape(groups, rows, width)
    entry_pre = (plain_dot(conv_flat, entry_dense) + entry_b).reshape(groups, rows, width)

    def gate_piece(rate_in, entry_in, conv_part, decay_in):
        return lru_gates(rate_in, entry_in, conv_part, decay_in, keep_mask, own_start)

    (decay_a, drive), gate_pull = jax.vjp(gate_piece, rate_pre, entry_pre, wide(conv_low), decay_full)
    cum_decay, local_state = local_scan(decay_a, drive, False)
    carry_in = carried_in(jnp.stack([cum_decay[:, -1], local_state[:, -1]]), False)
    hidden = local_state + cum_decay * carry_in[:, None]
    branch_pre = plain_dot(normed_low, branch_full) + branch_b
    branch_val, branch_pull = jax.vjp(gelu_tanh, branch_pre)
    merged = low(hidden.reshape(groups * rows, width) * branch_val)

    out_part = low(against_rows(merged, out_full)).reshape(groups, rows, model)
    inputs = wide(own_tokens)
    residual = inputs + scatter_batch(out_part) + out_b
    scale_two = inv_root(residual)
    normed_two = low(residual * scale_two * mlp_scale)
    normed_two_all = jnp.concatenate(gather_batch(normed_two), axis=0)

    two_pre = plain_dot(normed_two_all, two_full)
    gate_pre, up_pre = two_pre[:, :hidden_w], two_pre[:, hidden_w:]
    gate_act, gelu_pull = jax.vjp(gelu_tanh, gate_pre)
    activated = low(gate_act * up_pre)
    down_term = low(outer_sum(grad_all, activated))
    down_parts = join_columns(scatter_seq(down_term, jnp.bfloat16))
    act_grad = plain_dot(grad_all, down_full)
    gate_grad = low(gelu_pull(act_grad * up_pre)[0])
    up_grad = low(act_grad * gate_act)
    two_grad = jnp.concatenate([gate_grad, up_grad], axis=1)
    two_part = low(against_rows(two_grad, two_full))
    normed_two_grad = scatter_batch(two_part.reshape(groups, rows, model))
    two_term = low(outer_sum(normed_two_all, two_grad))
    two_share = scatter_seq(two_term, jnp.bfloat16)
    gate_parts = join_columns(two_share[:, :hidden_w])
    up_parts = join_columns(two_share[:, hidden_w:])
    residual_part, mlp_gain_term = norm_backward(residual, scale_two, mlp_scale, normed_two_grad)
    residual_grad = wide(grad_low) + residual_part
    mix_low = low(residual_grad)
    mix_all = jnp.concatenate(gather_batch(mix_low), axis=0)
    out_bias_term = jnp.sum(wide(mix_low), axis=0)
    block_part = low(against_rows(activated, down_full)).reshape(groups, rows, model)
    block_out = reorder(low(residual + scatter_batch(block_part)), order, True)

    merged_grad = plain_dot(mix_all, out_full)
    out_term = low(outer_sum(mix_all, merged))
    out_parts = join_columns(scatter_seq(out_term, jnp.bfloat16))
    state_grad = (merged_grad * branch_val).reshape(groups, rows, width)
    branch_low = low(branch_pull(merged_grad * hidden.reshape(groups * rows, width))[0])
    branch_term = low(outer_sum(normed_low, branch_low))
    branch_parts = join_columns(scatter_seq(branch_term, jnp.bfloat16))
    next_decay = jnp.concatenate([decay_a[:, 1:], jnp.ones((groups, 1, width), jnp.float32)], axis=1)
    cum_back, local_adjoint = local_scan(next_decay, state_grad, True)
    first_decay = decay_a[:, 0]
    adjoint_in = carried_in(
        jnp.stack([first_decay * cum_back[:, 0], first_decay * local_adjoint[:, 0]]), True
    )
    adjoint = local_adjoint + cum_back * adjoint_in[:, None]
    prev_state = jnp.concatenate([carry_in[:, None], hidden[:, :-1]], axis=1)
    rate_grad, entry_grad, conv_direct, decay_term = gate_pull((adjoint * prev_state, adjoint))
    rate_low = low(rate_grad).reshape(groups * rows, width)
    entry_low = low(entry_grad).reshape(groups * rows, width)
    conv_grad = (
        conv_direct.reshape(groups * rows, width)
        + against_rows(rate_low, rate_dense)
        + against_rows(entry_low, entry_dense)
    )
    conv_grad_low = low(conv_grad).reshape(groups, rows, width)
    after_rim = lax.ppermute(
        conv_grad_low[:, :RIM], "seq", [(i + 1, i) for i in range(seq - 1)]
    )[:, : tap_count - 1]
    conv_grad_f = wide(conv_grad_low)
    grad_ext = wide(jnp.concatenate([conv_grad_low, after_rim], axis=1))
    input_grad = jnp.zeros((groups, rows, width), jnp.float32)
    tap_terms = []
    for offset in range(tap_count):
        tap_terms.append(
            jnp.sum(conv_grad_f * valid(offset, False) * wide(behind(offset)), axis=(0, 1))
        )
        input_grad = (
            input_grad
            + tap_vals[offset] * grad_ext[:, offset : offset + rows] * valid(offset, True)
        )
    input_low = low(input_grad).reshape(groups * rows, width)
    mix_part = against_rows(branch_low, branch_full) + against_rows(input_low, input_full)
    mix_gain_term = jnp.sum(
        mix_part.reshape(groups, rows, model) * inputs_all[:, RIM:] * scale_all[:, RIM:], axis=(0, 1)
    )
    normed_grad = scatter_batch(low(mix_part).reshape(groups, rows, model))
    model_terms = jnp.stack([mix_gain_term, mlp_gain_term, out_bias_term], axis=1)
    model_terms = jnp.pad(model_terms, ((0, 0), (0, 125)))
    input_term = jnp.concatenate([outer_sum(normed_low, input_low), model_terms], axis=1)
    input_share = scatter_seq(low(input_term), jnp.bfloat16)
    input_parts = join_columns(input_share[:, :width])
    model_out = sum(wide(p) for p in join_columns(input_share[:, width:]))[:, :3]
    input_part, _ = norm_backward(inputs, scale_all[0, RIM:], mix_scale, normed_grad)
    tokens_grad = reorder(residual_grad + input_part, order, True)[None]

    rate_term = head_blocks(outer_sum(conv_flat, rate_low), heads, block_w)
    entry_term = head_blocks(outer_sum(conv_flat, entry_low), heads, block_w)

    def column_sum(values):
        return jnp.sum(wide(values), axis=0)

    channel_terms = jnp.stack(
        tap_terms
        + [
            column_sum(branch_low),
            column_sum(input_low),
            jnp.sum(conv_grad_f, axis=(0, 1)),
            column_sum(rate_low),
            column_sum(entry_low),
            decay_term,
        ],
        axis=1,
    )
    small = jnp.concatenate(
        [rate_term, entry_term, channel_terms, jnp.zeros((width, lane_pad), jnp.float32)], axis=1
    )
    first = low(small)
    rest = small - wide(first)
    second = low(rest)
    small = plain_dot(channels, first) + plain_dot(channels, second)
    channel_sum = scatter_seq(small, jnp.float32)
    vec_sum = channel_sum[:, 2 * block_w :]
    at = tap_count
    return (
        block_out[None],
        tokens_grad,
        model_out[:, 0],
        whole_rows(branch_parts),
        whole_rows(input_parts),
        vec_sum[:, at],
        vec_sum[:, at + 1],
        vec_sum[:, :tap_count],
        vec_sum[:, at + 2],
        channel_sum[:, :block_w],
        channel_sum[:, block_w : 2 * block_w],
        vec_sum[:, at + 3],
        vec_sum[:, at + 4],
        vec_sum[:, at + 5],
        whole_rows(out_parts),
        model_out[:, 2],
        model_out[:, 1],
        whole_rows(gate_parts),
        whole_rows(up_parts),
        whole_rows(down_parts),
    )


def solution(mesh):
    everywhere = ("batch", "seq")
    vector, matrix = P(everywhere), P(everywhere, None)
    block = P("batch", "seq", None)
    weights = (
        vector,
        matrix,
        matrix,
        vector,
        vector,
        matrix,
        vector,
        matrix,
        matrix,
        vector,
        vector,
        vector,
        matrix,
        vector,
        vector,
        matrix,
        matrix,
        matrix,
    )
    return jax.shard_map(
        shards,
        mesh=mesh,
        in_specs=(block, P("batch", None), block) + weights,
        out_specs=(block, block) + weights,
        check_vma=False,
    )
```

```python
import functools

import jax
import jax.numpy as jnp
from jax import lax
from jax.experimental import pallas as pl
from jax.experimental.pallas import tpu as pltpu
from jax.sharding import PartitionSpec as P

RIM = 16


def plain_dot(first_op, second_op):
    return jnp.dot(first_op, second_op, preferred_element_type=jnp.float32)


def outer_sum(first_op, second_op):
    return lax.dot_general(
        first_op, second_op, (((0,), (0,)), ((), ())), preferred_element_type=jnp.float32
    )


def against_rows(first_op, second_op):
    return lax.dot_general(
        first_op, second_op, (((1,), (1,)), ((), ())), preferred_element_type=jnp.float32
    )


def gelu_tanh(values):
    return jax.nn.gelu(values, approximate=True)


def low(values):
    return values.astype(jnp.bfloat16)


def wide(values):
    return values.astype(jnp.float32)


def across_batch(block, flip):
    return lax.ppermute(block, "batch", [(i, i ^ flip) for i in range(lax.axis_size("batch"))])


def flip_x(block):
    return lax.ppermute(block, "seq", [(i, i ^ 1) for i in range(lax.axis_size("seq"))])


def along_z(block, hops):
    return lax.ppermute(block, "seq", [(2 * a + x, 2 * b + x) for a, b in hops for x in range(2)])


def flip_z(block, by):
    return along_z(block, [(i, i ^ by) for i in range(lax.axis_size("seq") // 2)])


def after(value, *others):
    return lax.optimization_barrier((value, *others))[0]


def here_x():
    return lax.rem(lax.axis_index("seq"), 2)


def in_x_order(mine, other):
    first = here_x() == 0
    return [jnp.where(first, mine, other), jnp.where(first, other, mine)]


def across(block, flip_b, flip_s):
    if flip_b == 0 and flip_s == 0:
        return block
    size_b, size_s = lax.axis_size("batch"), lax.axis_size("seq")
    route = [
        (i * size_s + j, (i ^ flip_b) * size_s + (j ^ flip_s))
        for i in range(size_b)
        for j in range(size_s)
    ]
    return lax.ppermute(block, ("batch", "seq"), route)


EIGHT = [(k, j) for j in range(2) for k in (2, 1, 3, 0)]


def place_kernel(place_of, *refs):
    out_ref = refs[-1]
    for i, ref in enumerate(refs[:-1]):
        out_ref[place_of(i)] = ref[...]


def place(parts, place_of):
    return pl.pallas_call(
        functools.partial(place_kernel, place_of),
        out_shape=jax.ShapeDtypeStruct((len(parts),) + parts[0].shape, parts[0].dtype),
        compiler_params=pltpu.CompilerParams(vmem_limit_bytes=32 * 2**20),
        cost_estimate=pl.CostEstimate(
            flops=0, bytes_accessed=4 * len(parts) * parts[0].size, transcendentals=0
        ),
    )(*parts)


def swap_eight(blocks, *meanwhile):
    x, b = here_x(), lax.axis_index("batch")
    got = []
    for k, j in EIGHT:
        block = lax.dynamic_index_in_dim(blocks, (x ^ j) * 4 + (b ^ k), 0, False)
        got.append(across(block, k, j))

    def place_of(i):
        k, j = EIGHT[i]
        return (lax.rem(lax.axis_index("seq"), 2) ^ j) * 4 + (lax.axis_index("batch") ^ k)

    return place(after(got, *meanwhile), place_of)


def gather_eight(block, *meanwhile):
    half = block.shape[0] // 2
    over_y = across_batch(block, 2)
    over_x = flip_x(block)
    over_y, over_x = after((over_y, over_x), *meanwhile)
    both_a = flip_x(over_y[:half])
    both_b = across_batch(over_x[half:], 2)
    here = [block, over_x, over_y, both_a, both_b]
    return here + [across_batch(part, 1) for part in here], over_y, both_b


def scatter_eight(mine, theirs, first_work=(), last_work=()):
    got = across_batch(theirs, 1)
    own, over_x, over_y, both = [wide(mine[k]) + wide(got[k]) for k in ((0, 0), (0, 1), (1, 0), (1, 1))]
    half = both.shape[0] // 2
    via_x = flip_x(low(both[:half]))
    via_y = across_batch(low(both[half:]), 2)
    via_x, via_y = after((via_x, via_y), *first_work)
    over_y = jnp.concatenate([over_y[:half] + wide(via_x), over_y[half:]], axis=0)
    over_x = jnp.concatenate([over_x[:half], over_x[half:] + wide(via_y)], axis=0)
    last = across_batch(low(over_y), 2), flip_x(low(over_x))
    last = after(last, *last_work)
    return own + wide(last[0]) + wide(last[1])


def z_lines():
    count = lax.axis_size("seq")
    return [list(range(x, count, 2)) for x in range(2)]


def gather_z(block):
    return lax.all_gather(block, "seq", axis_index_groups=z_lines(), axis=0, tiled=True)


def gather_z_now(block):
    count = lax.axis_size("seq") // 2
    return [block if k == 0 else flip_z(block, k) for k in range(count)]


def in_z_order(blocks):
    return place(blocks, lambda i: (lax.axis_index("seq") // 2) ^ i)


def scatter_z(term):
    return lax.psum_scatter(
        term, "seq", scatter_dimension=0, axis_index_groups=z_lines(), tiled=True
    )


def cut_kernel(width, full, extra, *refs):
    out_ref = refs[-1]
    ins = refs[:-1]
    rows = out_ref.shape[1]
    for i in range(out_ref.shape[0]):
        first = (i % 4 * 2 + i // 4) * width
        pieces = []
        for n, ref in enumerate(ins[: len(ins) - extra]):
            piece = ref[:, first : first + width]
            if full > width:
                tail = jnp.zeros((rows, full - width), piece.dtype)
                if extra and n == len(ins) - extra - 1:
                    tail = ins[-1][:, : full - width]
                piece = jnp.concatenate([piece, tail], axis=1)
            pieces.append(piece)
        out_ref[i] = jnp.concatenate(pieces, axis=1)


def cut(weights, full, common=None):
    rows = weights[0].shape[0]
    ins = list(weights) + ([] if common is None else [common])
    return pl.pallas_call(
        functools.partial(cut_kernel, weights[0].shape[1] // 8, full, 0 if common is None else 1),
        out_shape=jax.ShapeDtypeStruct((8, rows, full * len(weights)), weights[0].dtype),
        compiler_params=pltpu.CompilerParams(vmem_limit_bytes=32 * 2**20),
        cost_estimate=pl.CostEstimate(
            flops=0, bytes_accessed=4 * weights[0].size * len(weights), transcendentals=0
        ),
    )(*ins)


def whole_rows(parts, first, last):
    return wide(
        jnp.concatenate([parts[i * 4 + j, :, first:last] for j in range(4) for i in range(2)], axis=1)
    )


def in_run_order(own, other, reverse):
    first, second = in_x_order(own, other)
    return (second, first) if reverse else (first, second)


def carried_in(decay, state, reverse):
    z = lax.axis_index("seq") // 2
    count = lax.axis_size("seq") // 2
    decay_one, decay_two = in_run_order(decay[:, 0], decay[:, 1], reverse)
    state_one, state_two = in_run_order(state[:, 0], state[:, 1], reverse)
    total_a, total_b = decay_one * decay_two, decay_two * state_one + state_two
    enter_a, enter_b = jnp.ones_like(total_a), jnp.zeros_like(total_b)
    bit = 1
    while bit < count:
        got = flip_z(jnp.stack([total_a, total_b]), bit)
        got_a, got_b = got[0], got[1]
        theirs_first = ((z & bit) == 0) if reverse else ((z & bit) != 0)
        enter_b = jnp.where(theirs_first, enter_a * got_b + enter_b, enter_b)
        enter_a = jnp.where(theirs_first, enter_a * got_a, enter_a)
        total_b = jnp.where(theirs_first, total_a * got_b + total_b, got_a * total_b + got_b)
        total_a = total_a * got_a
        bit *= 2
    second = decay_one * enter_b + state_one
    return jnp.stack(in_run_order(enter_b, second, reverse), axis=1)


def scan_kernel(reverse, a_ref, b_ref, cum_ref, out_ref):
    groups, rows, lanes = a_ref.shape
    tiles = rows // 8
    row = lax.broadcasted_iota(jnp.int32, (8, lanes), 0)

    def step(i, carry):
        tile = tiles - 1 - i if reverse else i
        at = pl.ds(pl.multiple_of(tile * 8, 8), 8)
        after = []
        for g in range(groups):
            a, b = a_ref[g, at, :], b_ref[g, at, :]
            for shift in (1, 2, 4):
                by = 8 - shift if reverse else shift
                ok = row < 8 - shift if reverse else row >= shift
                a_far = jnp.where(ok, pltpu.roll(a, by, 0), 1.0)
                b_far = jnp.where(ok, pltpu.roll(b, by, 0), 0.0)
                b = b + a * b_far
                a = a * a_far
            cum, state = carry[g]
            b = b + a * state
            a = a * cum
            cum_ref[g, at, :] = a
            out_ref[g, at, :] = b
            last = 0 if reverse else 7
            after.append(
                (
                    jnp.broadcast_to(a[last : last + 1], (8, lanes)),
                    jnp.broadcast_to(b[last : last + 1], (8, lanes)),
                )
            )
        return tuple(after)

    start = tuple(
        (jnp.ones((8, lanes), jnp.float32), jnp.zeros((8, lanes), jnp.float32))
        for _ in range(groups)
    )
    lax.fori_loop(0, tiles, step, start)


def local_scan(decay, drive, reverse):
    groups, rows, width = decay.shape
    lanes = 128 if width % 128 == 0 else width
    spec = pl.BlockSpec((groups, rows, lanes), lambda i: (0, 0, i))
    shape = jax.ShapeDtypeStruct(decay.shape, jnp.float32)
    return pl.pallas_call(
        functools.partial(scan_kernel, reverse),
        grid=(width // lanes,),
        in_specs=[spec, spec],
        out_specs=[spec, spec],
        out_shape=[shape, shape],
        cost_estimate=pl.CostEstimate(
            flops=20 * decay.size, bytes_accessed=16 * decay.size, transcendentals=0
        ),
    )(decay, drive)


def doc_layout(lengths, first_pos, span_count):
    second = lengths[:, 0:1]
    third = second + lengths[:, 1:2]
    places = first_pos + lax.broadcasted_iota(jnp.int32, (lengths.shape[0], span_count), 1)
    begins = jnp.where(places >= third, third, jnp.where(places >= second, second, 0))
    return places, places == begins, begins


def lru_gates(rate_in, entry_in, conv_in, decay_in, keep_mask, start_mask):
    rate_sig = jax.nn.sigmoid(rate_in)
    entry_sig = jax.nn.sigmoid(entry_in)
    log_decay = -8.0 * rate_sig * jax.nn.softplus(-decay_in)
    drive_scale = jnp.where(start_mask, 1.0, jnp.sqrt(-jnp.expm1(2.0 * log_decay)))
    return (jnp.exp(log_decay) * keep_mask, drive_scale * entry_sig * conv_in)


def inv_root(values):
    return lax.rsqrt(jnp.mean(values * values, axis=-1, keepdims=True) + 1e-06)


def norm_backward(values, scale, gain_vec, incoming):
    weighted = incoming * gain_vec
    inner_mean = jnp.mean(weighted * values, axis=-1, keepdims=True)
    return (
        scale * weighted - values * scale * scale * scale * inner_mean,
        jnp.sum(incoming * values * scale, axis=0),
    )


def head_diagonal(blocks, heads, width):
    size = blocks.shape[0]
    own = lax.broadcasted_iota(jnp.int32, (size, size), 0) // width
    at = lax.broadcasted_iota(jnp.int32, (size, size), 1) // width
    copies = jnp.tile(blocks, (1, heads))
    copies = jnp.pad(copies, ((0, 0), (0, size - heads * width)))
    return jnp.where(own == at, copies, jnp.zeros((), blocks.dtype))


def head_blocks(dense, width):
    size = dense.shape[0]
    own = lax.broadcasted_iota(jnp.int32, (size, size), 0) // width
    at = lax.broadcasted_iota(jnp.int32, (size, size), 1) // width
    pick = lax.broadcasted_iota(jnp.int32, (size, width), 0) % width
    pick = pick == lax.broadcasted_iota(jnp.int32, (size, width), 1)
    return plain_dot(low(jnp.where(own == at, dense, 0.0)), pick.astype(jnp.bfloat16))


def order_matrix(seq, own_d, zero):
    size = 4 * seq * own_d
    d = lax.broadcasted_iota(jnp.int32, (size, size), 0) + zero
    at = lax.broadcasted_iota(jnp.int32, (size, size), 1)
    place_b, rest = d // (seq * own_d), d % (seq * own_d)
    row = (rest // own_d * 4 + place_b) * own_d + rest % own_d
    return (row == at).astype(jnp.bfloat16)


def reorder(values, matrix, back=False):
    dot = against_rows if back else plain_dot
    if values.dtype == jnp.bfloat16:
        return low(dot(values, matrix))
    first = low(values)
    both = dot(jnp.concatenate([first, low(values - wide(first))], axis=0), matrix)
    return both[: values.shape[0]] + both[values.shape[0] :]


def shards(
    tokens,
    doc_lengths,
    out_grad,
    mix_gain,
    branch_weight,
    input_weight,
    branch_bias,
    input_bias,
    conv_taps,
    conv_bias,
    rate_weight,
    entry_weight,
    rate_bias,
    entry_bias,
    decay_param,
    out_weight,
    out_bias,
    mlp_gain,
    gate_weight,
    up_weight,
    down_weight,
):
    seq = lax.axis_size("seq")
    s = lax.axis_index("seq")
    z_count = seq // 2
    rows, model = tokens.shape[1:]
    block_w = rate_weight.shape[1]
    tap_count = conv_taps.shape[1]
    width = branch_weight.shape[1] // 8
    full_w = -(-width // 128) * 128
    hidden_w = gate_weight.shape[1] // 8
    heads = width // block_w
    own_r = conv_bias.shape[0]
    own_d = mix_gain.shape[0]
    groups, blocks = 4, 8
    every = blocks * rows

    pack_w = -(-(2 * block_w + tap_count + 6) // 128) * 128
    lengths = jnp.concatenate([doc_lengths] + [across_batch(doc_lengths, k) for k in (2, 1, 3)], 0)
    model_vec = jnp.stack([mix_gain, mlp_gain, out_bias], axis=1)
    model_vec = jnp.pad(model_vec, ((0, 0), (0, 125)))
    rec_cut = cut([branch_weight, out_weight, input_weight], full_w, model_vec)
    weight_rows = 8 * own_d
    rec_rows = swap_eight(rec_cut).reshape(weight_rows, -1)

    order = order_matrix(seq, own_d, after(s, rec_cut) * 0)
    own_tokens = reorder(tokens[0], order)
    vectors = jnp.stack(
        [branch_bias, input_bias, conv_bias, rate_bias, entry_bias, decay_param], axis=1
    )
    pack = jnp.concatenate([after(rate_weight, rec_cut), entry_weight, conv_taps, vectors], axis=1)
    pack = jnp.pad(pack, ((0, 0), (0, pack_w - pack.shape[1])))
    pack = jnp.concatenate(in_x_order(pack, flip_x(pack)), axis=0)
    first = gather_z_now(jnp.concatenate([rec_rows[:, 2 * full_w :], pack], axis=0))
    tokens_parts, _, tokens_last = gather_eight(after(own_tokens, rec_rows, lengths))
    first = in_z_order(after(first, tokens_last))

    input_all = first[:, :weight_rows].reshape(model, full_w)
    pack_all = first[:, weight_rows:].reshape(-1, pack_w)
    model_full = wide(input_all[:, width : width + 3]).T
    mix_scale, mlp_scale, out_b = model_full[0], model_full[1], model_full[2]
    rec_full = gather_z(after(rec_rows[:, : 2 * full_w], tokens_last))
    branch_full, out_full = rec_full[:, :full_w], rec_full[:, full_w:]

    mlp_cut = cut(after((gate_weight, up_weight, down_weight), rec_rows), hidden_w)
    mlp_rows = swap_eight(after(mlp_cut, tokens_last)).reshape(weight_rows, -1)
    gate_full = gather_z(mlp_rows[:, :hidden_w])
    up_full = gather_z(mlp_rows[:, hidden_w : 2 * hidden_w])
    down_full = gather_z(mlp_rows[:, 2 * hidden_w :])
    two_full = jnp.concatenate([gate_full, up_full], axis=1)
    grad_low = reorder(after(out_grad[0], rec_rows), order)

    by_channel = lax.dynamic_slice_in_dim(pack_all, here_x() * width, width, 0)
    by_channel = jnp.pad(by_channel, ((0, full_w - width), (0, 0)))
    rate_dense = head_diagonal(by_channel[:, :block_w], heads, block_w)
    entry_dense = head_diagonal(by_channel[:, block_w : 2 * block_w], heads, block_w)
    channel_vec = wide(by_channel[:, 2 * block_w : 2 * block_w + tap_count + 6]).T
    tap_vals = channel_vec[:tap_count]
    branch_b, input_b, conv_b, rate_b, entry_b, decay_full = [
        channel_vec[tap_count + i] for i in range(6)
    ]
    layouts = [doc_layout(lengths, place * rows, rows + tap_count - 1) for place in (s, s ^ 1)]
    places, start_mask, begins = [
        jnp.stack([one, other], axis=1).reshape(blocks, -1) for one, other in zip(*layouts)
    ]
    own_start = start_mask[:, :rows, None]
    keep_mask = 1.0 - own_start.astype(jnp.float32)

    normed_low = [low(wide(part) * inv_root(wide(part)) * mix_scale) for part in tokens_parts]
    normed_low = lax.optimization_barrier(jnp.concatenate(normed_low, axis=0))
    own_channel = jnp.arange(full_w) < width
    input_full = jnp.where(own_channel, input_all, jnp.zeros((), jnp.bfloat16))
    conv_in = low(plain_dot(normed_low, input_full) + input_b).reshape(groups, 2, rows, full_w)
    x = here_x()

    def rims(values, first, last, hops):
        edge = values[:, :, first:last]
        forward = hops[0][1] > hops[0][0]
        sent_block, near_block = in_x_order(edge[:, 0], edge[:, 1])
        if forward:
            sent_block, near_block = near_block, sent_block
        got = along_z(sent_block, hops)
        at_edge = x == 0 if forward else x == 1
        own_rim = jnp.where(at_edge, got, edge[:, 1])
        other_rim = jnp.where(at_edge, edge[:, 0], got)
        return jnp.stack([own_rim, other_rim], axis=1)

    before = rims(conv_in, rows - RIM, rows, [(i, i + 1) for i in range(z_count - 1)])
    conv_in = jnp.concatenate([before, conv_in], axis=2).reshape(blocks, RIM + rows, full_w)

    def behind(offset):
        return conv_in[:, RIM - offset : RIM - offset + rows]

    def valid(offset, ahead):
        at = slice(offset, offset + rows) if ahead else slice(0, rows)
        return wide(places[:, at] - offset >= begins[:, at])[:, :, None]

    conv_val = jnp.zeros((blocks, rows, full_w), jnp.float32) + conv_b
    for offset in range(tap_count):
        conv_val = conv_val + tap_vals[offset] * wide(behind(offset)) * valid(offset, False)
    conv_low = low(conv_val)
    conv_flat = after(conv_low, rec_full).reshape(every, full_w)
    rate_pre = (plain_dot(conv_flat, rate_dense) + rate_b).reshape(blocks, rows, full_w)
    entry_pre = (plain_dot(conv_flat, entry_dense) + entry_b).reshape(blocks, rows, full_w)

    def gate_piece(rate_in, entry_in, conv_part, decay_in):
        return lru_gates(rate_in, entry_in, conv_part, decay_in, keep_mask, own_start)

    (decay_a, drive), gate_pull = jax.vjp(gate_piece, rate_pre, entry_pre, wide(conv_low), decay_full)
    cum_decay, local_state = local_scan(after(decay_a, mlp_rows), drive, False)
    grad_parts, grad_over, _ = gather_eight(after(grad_low, mlp_rows), cum_decay)
    grad_all = jnp.concatenate(grad_parts, axis=0)
    carry_in = carried_in(
        cum_decay[:, -1].reshape(groups, 2, full_w), local_state[:, -1].reshape(groups, 2, full_w), False
    ).reshape(blocks, full_w)
    hidden = local_state + cum_decay * after(carry_in, grad_over)[:, None]
    branch_pre = plain_dot(normed_low, branch_full) + branch_b
    branch_val, branch_pull = jax.vjp(gelu_tanh, branch_pre)
    merged = after(low(hidden.reshape(every, full_w) * branch_val), gate_full)

    def token_terms(part, weight):
        return low(against_rows(part, weight)).reshape(2, 2, rows, model)

    def summed(values, weight, first_work=(), last_work=()):
        theirs = token_terms(values[every // 2 :], weight)
        return scatter_eight(token_terms(values[: every // 2], weight), theirs, first_work, last_work)

    inputs = wide(own_tokens)
    residual = inputs + summed(merged, out_full, (grad_all,), (up_full,)) + out_b
    scale_two = inv_root(residual)
    normed_two = low(residual * scale_two * mlp_scale)
    normed_two_all = jnp.concatenate(gather_eight(normed_two)[0], axis=0)

    two_pre = plain_dot(after(normed_two_all, down_full), two_full)
    gate_pre, up_pre = two_pre[:, :hidden_w], two_pre[:, hidden_w:]
    gate_act, gelu_pull = jax.vjp(gelu_tanh, gate_pre)
    activated = low(gate_act * up_pre)
    act_grad = plain_dot(grad_all, down_full)
    gate_grad = low(gelu_pull(act_grad * up_pre)[0])
    up_grad = low(act_grad * gate_act)
    two_grad = jnp.concatenate([gate_grad, up_grad], axis=1)
    down_term = low(outer_sum(grad_all, activated))
    two_term = low(outer_sum(normed_two_all, two_grad))
    down_share = scatter_z(down_term)
    normed_two_grad = summed(two_grad, two_full, (down_term,), (two_term, down_share))
    two_share = scatter_z(after(two_term, down_share))
    residual_part, mlp_gain_term = norm_backward(residual, scale_two, mlp_scale, normed_two_grad)
    residual_grad = wide(grad_low) + residual_part
    mix_low = low(residual_grad)
    out_bias_term = jnp.sum(wide(mix_low), axis=0)
    block_theirs = token_terms(activated[every // 2 :], down_full)
    block_mine = token_terms(activated[: every // 2], down_full)
    mix_parts, _, mix_last = gather_eight(mix_low, block_theirs, block_mine)
    mix_all = jnp.concatenate(mix_parts, axis=0)

    merged_grad = plain_dot(mix_all, out_full)
    state_grad = (merged_grad * branch_val).reshape(blocks, rows, full_w)
    next_decay = jnp.concatenate([decay_a[:, 1:], jnp.ones((blocks, 1, full_w), jnp.float32)], axis=1)
    cum_back, local_adjoint = local_scan(next_decay, state_grad, True)
    first_decay = decay_a[:, 0]
    adjoint_in = carried_in(
        (first_decay * cum_back[:, 0]).reshape(groups, 2, full_w),
        (first_decay * local_adjoint[:, 0]).reshape(groups, 2, full_w),
        True,
    ).reshape(blocks, full_w)
    out_term = low(outer_sum(mix_all, merged))
    branch_low = low(branch_pull(merged_grad * hidden.reshape(every, full_w))[0])
    branch_term = outer_sum(normed_low, branch_low)

    adjoint = local_adjoint + cum_back * adjoint_in[:, None]
    prev_state = jnp.concatenate([carry_in[:, None], hidden[:, :-1]], axis=1)
    rate_grad, entry_grad, conv_direct, decay_term = gate_pull((adjoint * prev_state, adjoint))
    rate_low = low(rate_grad).reshape(every, full_w)
    entry_low = low(entry_grad).reshape(every, full_w)
    block_sum = scatter_eight(block_mine, after(block_theirs, mix_last), (adjoint_in,), (rate_low,))
    block_out = reorder(low(residual + block_sum), order, True)
    conv_grad = (
        conv_direct.reshape(every, full_w)
        + against_rows(after(rate_low, two_share), rate_dense)
        + against_rows(entry_low, entry_dense)
    )
    conv_grad_low = low(conv_grad).reshape(groups, 2, rows, full_w)
    after_rim = rims(conv_grad_low, 0, RIM, [(i + 1, i) for i in range(z_count - 1)])
    grad_ext = wide(jnp.concatenate([conv_grad_low, after_rim[:, :, : tap_count - 1]], axis=2))
    grad_ext = grad_ext.reshape(blocks, rows + tap_count - 1, full_w)
    conv_grad_f = wide(conv_grad_low).reshape(blocks, rows, full_w)
    rec_share = scatter_z(after(jnp.concatenate([out_term, low(branch_term)], axis=1), two_share))
    input_grad = jnp.zeros((blocks, rows, full_w), jnp.float32)
    tap_terms = []
    for offset in range(tap_count):
        tap_terms.append(
            jnp.sum(conv_grad_f * valid(offset, False) * wide(behind(offset)), axis=(0, 1))
        )
        input_grad = (
            input_grad
            + tap_vals[offset] * grad_ext[:, offset : offset + rows] * valid(offset, True)
        )
    input_low = after(low(input_grad), block_sum).reshape(every, full_w)
    both_low = jnp.concatenate([branch_low, input_low], axis=1)
    both_full = jnp.concatenate([branch_full, input_full], axis=1)
    input_term = outer_sum(normed_low, input_low)
    mix_gain_term = branch_term * wide(branch_full) + input_term * wide(input_full)
    mix_gain_term = jnp.sum(mix_gain_term, axis=1) / mix_scale
    model_terms = jnp.stack([mix_gain_term, mlp_gain_term, out_bias_term], axis=1)
    model_terms = jnp.pad(model_terms, ((0, 0), (0, full_w - width - 3)))
    input_block = low(jnp.concatenate([input_term[:, :width], model_terms], axis=1))

    rate_term = head_blocks(outer_sum(conv_flat, rate_low), block_w)
    entry_term = head_blocks(outer_sum(conv_flat, entry_low), block_w)

    def column_sum(values):
        return jnp.sum(wide(values), axis=0)

    channel_terms = jnp.stack(
        tap_terms
        + [
            column_sum(branch_low),
            column_sum(input_low),
            jnp.sum(conv_grad_f, axis=(0, 1)),
            column_sum(rate_low),
            column_sum(entry_low),
            decay_term,
        ],
        axis=1,
    )
    small = low(jnp.concatenate([rate_term, entry_term, channel_terms], axis=1))[:width]
    small = jnp.pad(small, ((0, 0), (0, pack_w - small.shape[1])))
    small = lax.dynamic_update_slice_in_dim(
        jnp.zeros((2 * width, pack_w), jnp.bfloat16), small, x * width, 0
    )
    input_block = jnp.concatenate(
        [input_block.reshape(z_count, weight_rows, -1), small.reshape(z_count, 2 * own_r, -1)], axis=1
    ).reshape(-1, pack_w)
    input_share = scatter_z(input_block)
    normed_grad = summed(both_low, both_full, (input_term, rec_share), (input_block,))
    mlp_share = jnp.concatenate([two_share, down_share], axis=1)
    two_back = swap_eight(after(mlp_share, normed_grad).reshape(8, own_d, -1))
    input_part, _ = norm_backward(inputs, inv_root(inputs), mix_scale, normed_grad)
    tokens_grad = reorder(residual_grad + input_part, order, True)[None]
    rec_back = swap_eight(
        jnp.concatenate([rec_share, input_share[:weight_rows]], axis=1).reshape(8, own_d, -1),
        normed_grad,
    )
    small_share = after(input_share[weight_rows:], normed_grad).reshape(2, own_r, pack_w)
    channel_sum = wide(lax.dynamic_index_in_dim(small_share, x, 0, False)) + wide(
        flip_x(lax.dynamic_index_in_dim(small_share, 1 - x, 0, False))
    )
    vec_sum = channel_sum[:, 2 * block_w :]
    model_at = 2 * full_w + width
    model_out = jnp.sum(wide(rec_back[:, :, model_at : model_at + 3]), axis=0)
    at = tap_count
    return (
        block_out[None],
        tokens_grad,
        model_out[:, 0],
        whole_rows(rec_back, full_w, full_w + width),
        whole_rows(rec_back, 2 * full_w, 2 * full_w + width),
        vec_sum[:, at],
        vec_sum[:, at + 1],
        vec_sum[:, :tap_count],
        vec_sum[:, at + 2],
        channel_sum[:, :block_w],
        channel_sum[:, block_w : 2 * block_w],
        vec_sum[:, at + 3],
        vec_sum[:, at + 4],
        vec_sum[:, at + 5],
        whole_rows(rec_back, 0, width),
        model_out[:, 2],
        model_out[:, 1],
        whole_rows(two_back, 0, hidden_w),
        whole_rows(two_back, hidden_w, 2 * hidden_w),
        whole_rows(two_back, 2 * hidden_w, 3 * hidden_w),
    )


def solution(mesh):
    everywhere = ("batch", "seq")
    vector, matrix = P(everywhere), P(everywhere, None)
    block = P("batch", "seq", None)
    weights = (
        vector,
        matrix,
        matrix,
        vector,
        vector,
        matrix,
        vector,
        matrix,
        matrix,
        vector,
        vector,
        vector,
        matrix,
        vector,
        vector,
        matrix,
        matrix,
        matrix,
    )
    return jax.shard_map(
        shards,
        mesh=mesh,
        in_specs=(block, P("batch", None), block) + weights,
        out_specs=(block, block) + weights,
        check_vma=False,
    )
```

```python
import functools

import jax
import jax.numpy as jnp
from jax import lax
from jax.experimental import pallas as pl
from jax.experimental.pallas import tpu as pltpu
from jax.sharding import Mesh
from jax.sharding import PartitionSpec as P

RIM = 16


def plain_dot(first_op, second_op):
    return jnp.dot(first_op, second_op, preferred_element_type=jnp.float32)


def outer_sum(first_op, second_op):
    return lax.dot_general(
        first_op, second_op, (((0,), (0,)), ((), ())), preferred_element_type=jnp.float32
    )


def against_rows(first_op, second_op):
    return lax.dot_general(
        first_op, second_op, (((1,), (1,)), ((), ())), preferred_element_type=jnp.float32
    )


def gelu_tanh(values):
    return jax.nn.gelu(values, approximate=True)


def low(values):
    return values.astype(jnp.bfloat16)


def wide(values):
    return values.astype(jnp.float32)


def across_batch(block, flip):
    return lax.ppermute(block, "batch", [(i, i ^ flip) for i in range(lax.axis_size("batch"))])


def flip_x(block):
    return lax.ppermute(block, "x", [(0, 1), (1, 0)])


def along_z(block, hops):
    return lax.ppermute(block, "z", hops)


def flip_z(block, by):
    return along_z(block, [(i, i ^ by) for i in range(lax.axis_size("z"))])


def after(value, *others):
    return lax.optimization_barrier((value, *others))[0]


def here_x():
    return lax.axis_index("x")


def in_x_order(mine, other):
    first = here_x() == 0
    return [jnp.where(first, mine, other), jnp.where(first, other, mine)]


def across(block, flip_b, flip_xs):
    if flip_b == 0 and flip_xs == 0:
        return block
    places = range(2 * lax.axis_size("batch"))
    return lax.ppermute(block, ("batch", "x"), [(i, i ^ (2 * flip_b + flip_xs)) for i in places])


EIGHT = [(k, j) for j in range(2) for k in (2, 1, 3, 0)]


def place_kernel(place_of, *refs):
    out_ref = refs[-1]
    for i, ref in enumerate(refs[:-1]):
        out_ref[place_of(i)] = ref[...]


def place(parts, place_of):
    return pl.pallas_call(
        functools.partial(place_kernel, place_of),
        out_shape=jax.ShapeDtypeStruct((len(parts),) + parts[0].shape, parts[0].dtype),
        compiler_params=pltpu.CompilerParams(vmem_limit_bytes=32 * 2**20),
        cost_estimate=pl.CostEstimate(
            flops=0, bytes_accessed=4 * len(parts) * parts[0].size, transcendentals=0
        ),
    )(*parts)


def join_kernel(count, place_of, *refs):
    ins, outs = refs[:-count], refs[-count:]
    width = ins[0].shape[1] // count
    for i, ref in enumerate(ins):
        place = place_of(i)
        first = pl.multiple_of((place % 4 * 2 + place // 4) * width, 128)
        for n, out in enumerate(outs):
            out[:, pl.ds(first, width)] = ref[:, n * width : (n + 1) * width].astype(jnp.float32)


def join(parts, place_of, count):
    rows, width = parts[0].shape
    shape = jax.ShapeDtypeStruct((rows, 8 * width // count), jnp.float32)
    return pl.pallas_call(
        functools.partial(join_kernel, count, place_of),
        out_shape=[shape] * count,
        compiler_params=pltpu.CompilerParams(vmem_limit_bytes=32 * 2**20),
        cost_estimate=pl.CostEstimate(
            flops=0, bytes_accessed=48 * rows * width, transcendentals=0
        ),
    )(*parts)


def swap_eight(blocks, *meanwhile, joined=0):
    x, b = here_x(), lax.axis_index("batch")
    got = []
    for k, j in EIGHT:
        block = lax.dynamic_index_in_dim(blocks, (x ^ j) * 4 + (b ^ k), 0, False)
        got.append(across(block, k, j))

    def place_of(i):
        k, j = EIGHT[i]
        return (here_x() ^ j) * 4 + (lax.axis_index("batch") ^ k)

    got = after(got, *meanwhile)
    return join(got, place_of, joined) if joined else place(got, place_of)


def gather_eight(block, *meanwhile):
    half = block.shape[0] // 2
    over_y = across_batch(block, 2)
    over_x = flip_x(block)
    over_y, over_x = after((over_y, over_x), *meanwhile)
    both_a = flip_x(over_y[:half])
    both_b = across_batch(over_x[half:], 2)
    here = [block, over_x, over_y, both_a, both_b]
    return here + [across_batch(part, 1) for part in here], over_y, (both_a, both_b)


def scatter_first(theirs):
    return [across_batch(theirs[k], 1) for k in range(4)]


def scatter_diagonal(mine, got):
    both = wide(mine[3]) + wide(got[3])
    half = both.shape[0] // 2
    return flip_x(low(both[:half])), across_batch(low(both[half:]), 2)


def scatter_last(mine, got, ways):
    mine, got = after((mine, got), ways)
    over_x, over_y = wide(mine[1]) + wide(got[1]), wide(mine[2]) + wide(got[2])
    half = over_x.shape[0] // 2
    over_y = jnp.concatenate([over_y[:half] + wide(ways[0]), over_y[half:]], axis=0)
    over_x = jnp.concatenate([over_x[:half], over_x[half:] + wide(ways[1])], axis=0)
    return across_batch(low(over_y), 2), flip_x(low(over_x))


def scatter_sum(mine, got, last):
    mine, got = after((mine[0], got[0]), last)
    return wide(mine) + wide(got) + wide(last[0]) + wide(last[1])


def gather_z(block):
    return lax.all_gather(block, "z", axis=0, tiled=True)


def gather_z_now(block):
    return [block if k == 0 else flip_z(block, k) for k in range(lax.axis_size("z"))]


def in_z_order(blocks):
    return place(blocks, lambda i: lax.axis_index("z") ^ i)


def scatter_z(term):
    return lax.psum_scatter(term, "z", scatter_dimension=0, tiled=True)


def cut_kernel(width, full, extra, *refs):
    out_ref = refs[-1]
    ins = refs[:-1]
    rows = out_ref.shape[1]
    for i in range(out_ref.shape[0]):
        first = (i % 4 * 2 + i // 4) * width
        pieces = []
        for n, ref in enumerate(ins[: len(ins) - extra]):
            piece = ref[:, first : first + width]
            if full > width:
                tail = jnp.zeros((rows, full - width), piece.dtype)
                if extra and n == len(ins) - extra - 1:
                    tail = ins[-1][:, : full - width]
                piece = jnp.concatenate([piece, tail], axis=1)
            pieces.append(piece)
        out_ref[i] = jnp.concatenate(pieces, axis=1)


def cut(weights, full, common=None):
    rows = weights[0].shape[0]
    ins = list(weights) + ([] if common is None else [common])
    return pl.pallas_call(
        functools.partial(cut_kernel, weights[0].shape[1] // 8, full, 0 if common is None else 1),
        out_shape=jax.ShapeDtypeStruct((8, rows, full * len(weights)), weights[0].dtype),
        compiler_params=pltpu.CompilerParams(vmem_limit_bytes=32 * 2**20),
        cost_estimate=pl.CostEstimate(
            flops=0, bytes_accessed=4 * weights[0].size * len(weights), transcendentals=0
        ),
    )(*ins)


def whole_rows(parts, first, last):
    return wide(
        jnp.concatenate([parts[i * 4 + j, :, first:last] for j in range(4) for i in range(2)], axis=1)
    )


def in_run_order(own, other, reverse):
    first, second = in_x_order(own, other)
    return (second, first) if reverse else (first, second)


def carried_in(decay, state, reverse):
    z = lax.axis_index("z")
    count = lax.axis_size("z")
    decay_one, decay_two = in_run_order(decay[:, 0], decay[:, 1], reverse)
    state_one, state_two = in_run_order(state[:, 0], state[:, 1], reverse)
    total_a, total_b = decay_one * decay_two, decay_two * state_one + state_two
    enter_a, enter_b = jnp.ones_like(total_a), jnp.zeros_like(total_b)
    bit = 1
    while bit < count:
        got = flip_z(jnp.stack([total_a, total_b]), bit)
        got_a, got_b = got[0], got[1]
        theirs_first = ((z & bit) == 0) if reverse else ((z & bit) != 0)
        enter_b = jnp.where(theirs_first, enter_a * got_b + enter_b, enter_b)
        enter_a = jnp.where(theirs_first, enter_a * got_a, enter_a)
        total_b = jnp.where(theirs_first, total_a * got_b + total_b, got_a * total_b + got_b)
        total_a = total_a * got_a
        bit *= 2
    second = decay_one * enter_b + state_one
    return jnp.stack(in_run_order(enter_b, second, reverse), axis=1)


def scan_kernel(reverse, a_ref, b_ref, cum_ref, out_ref):
    groups, rows, lanes = a_ref.shape
    tiles = rows // 8
    row = lax.broadcasted_iota(jnp.int32, (8, lanes), 0)

    def step(i, carry):
        tile = tiles - 1 - i if reverse else i
        at = pl.ds(pl.multiple_of(tile * 8, 8), 8)
        after = []
        for g in range(groups):
            a, b = a_ref[g, at, :], b_ref[g, at, :]
            for shift in (1, 2, 4):
                by = 8 - shift if reverse else shift
                ok = row < 8 - shift if reverse else row >= shift
                a_far = jnp.where(ok, pltpu.roll(a, by, 0), 1.0)
                b_far = jnp.where(ok, pltpu.roll(b, by, 0), 0.0)
                b = b + a * b_far
                a = a * a_far
            cum, state = carry[g]
            b = b + a * state
            a = a * cum
            cum_ref[g, at, :] = a
            out_ref[g, at, :] = b
            last = 0 if reverse else 7
            after.append(
                (
                    jnp.broadcast_to(a[last : last + 1], (8, lanes)),
                    jnp.broadcast_to(b[last : last + 1], (8, lanes)),
                )
            )
        return tuple(after)

    start = tuple(
        (jnp.ones((8, lanes), jnp.float32), jnp.zeros((8, lanes), jnp.float32))
        for _ in range(groups)
    )
    lax.fori_loop(0, tiles, step, start)


def local_scan(decay, drive, reverse):
    groups, rows, width = decay.shape
    lanes = 128 if width % 128 == 0 else width
    spec = pl.BlockSpec((groups, rows, lanes), lambda i: (0, 0, i))
    shape = jax.ShapeDtypeStruct(decay.shape, jnp.float32)
    return pl.pallas_call(
        functools.partial(scan_kernel, reverse),
        grid=(width // lanes,),
        in_specs=[spec, spec],
        out_specs=[spec, spec],
        out_shape=[shape, shape],
        cost_estimate=pl.CostEstimate(
            flops=20 * decay.size, bytes_accessed=16 * decay.size, transcendentals=0
        ),
    )(decay, drive)


def mlp_kernel(place_ref, normed_ref, grad_ref, two_ref, down_ref, act_ref, placed_ref, out_ref):
    width = act_ref.shape[1]
    lane = 256 if width % 256 == 0 else width
    normed, grad = normed_ref[...], grad_ref[...]
    for first in range(0, width, lane):
        at, up_at = slice(first, first + lane), slice(width + first, width + first + lane)
        gate = plain_dot(normed, two_ref[:, at])
        up = plain_dot(normed, two_ref[:, up_at])
        act_grad = plain_dot(grad, down_ref[:, at])
        square = gate * gate
        slope = 0.7978845608028654
        bent = jnp.tanh(slope * gate * (1.0 + 0.044715 * square))
        half = 0.5 + 0.5 * bent
        act = half * gate
        act_slope = half + 0.5 * gate * (1.0 - bent * bent) * (slope * (1.0 + 0.134145 * square))
        activated = low(act * up)
        act_ref[:, at] = activated
        placed_ref[:, at] = activated
        out_ref[:, at] = low(act_grad * up * act_slope)
        out_ref[:, up_at] = low(act_grad * act)


def mlp(normed, grad, two_full, down_full, rows):
    count, model = normed.shape
    width = down_full.shape[1]
    here = 2 * lax.axis_index("batch") + here_x()
    order = jnp.arange(8, dtype=jnp.int32)
    place = (order // 4 * 2 + order // 2 % 2 * 4 + order % 2) ^ here.astype(jnp.int32)
    block = lambda columns: pl.BlockSpec((rows, columns), lambda i, place_ref: (i, 0))
    whole = lambda columns: pl.BlockSpec((model, columns), lambda i, place_ref: (0, 0))
    shape = lambda columns: jax.ShapeDtypeStruct((count, columns), jnp.bfloat16)
    return pl.pallas_call(
        mlp_kernel,
        grid_spec=pltpu.PrefetchScalarGridSpec(
            num_scalar_prefetch=1,
            grid=(count // rows,),
            in_specs=[block(model), block(model), whole(2 * width), whole(width)],
            out_specs=[
                block(width),
                pl.BlockSpec((rows, width), lambda i, place_ref: (place_ref[i], 0)),
                block(2 * width),
            ],
        ),
        out_shape=[shape(width), shape(width), shape(2 * width)],
        compiler_params=pltpu.CompilerParams(vmem_limit_bytes=56 * 2**20),
        cost_estimate=pl.CostEstimate(
            flops=6 * count * model * width,
            bytes_accessed=2 * (2 * count * model + 3 * model * width + 4 * count * width),
            transcendentals=count * width,
        ),
    )(place, normed, grad, two_full, down_full)


def doc_layout(lengths, first_pos, span_count):
    second = lengths[:, 0:1]
    third = second + lengths[:, 1:2]
    places = first_pos + lax.broadcasted_iota(jnp.int32, (lengths.shape[0], span_count), 1)
    begins = jnp.where(places >= third, third, jnp.where(places >= second, second, 0))
    return places, places == begins, begins


def lru_gates(rate_in, entry_in, conv_in, decay_in, keep_mask, start_mask):
    rate_sig = jax.nn.sigmoid(rate_in)
    entry_sig = jax.nn.sigmoid(entry_in)
    log_decay = -8.0 * rate_sig * jax.nn.softplus(-decay_in)
    drive_scale = jnp.where(start_mask, 1.0, jnp.sqrt(-jnp.expm1(2.0 * log_decay)))
    return (jnp.exp(log_decay) * keep_mask, drive_scale * entry_sig * conv_in)


def inv_root(values):
    return lax.rsqrt(jnp.mean(values * values, axis=-1, keepdims=True) + 1e-06)


def norm_backward(values, scale, gain_vec, incoming):
    weighted = incoming * gain_vec
    inner_mean = jnp.mean(weighted * values, axis=-1, keepdims=True)
    return (
        scale * weighted - values * scale * scale * scale * inner_mean,
        jnp.sum(incoming * values * scale, axis=0),
    )


def head_diagonal(blocks, heads, width):
    size = blocks.shape[0]
    own = lax.broadcasted_iota(jnp.int32, (size, size), 0) // width
    at = lax.broadcasted_iota(jnp.int32, (size, size), 1) // width
    copies = jnp.tile(blocks, (1, heads))
    copies = jnp.pad(copies, ((0, 0), (0, size - heads * width)))
    return jnp.where(own == at, copies, jnp.zeros((), blocks.dtype))


def head_blocks(dense, width):
    size = dense.shape[0]
    own = lax.broadcasted_iota(jnp.int32, (size, size), 0) // width
    at = lax.broadcasted_iota(jnp.int32, (size, size), 1) // width
    pick = lax.broadcasted_iota(jnp.int32, (size, width), 0) % width
    pick = pick == lax.broadcasted_iota(jnp.int32, (size, width), 1)
    return plain_dot(low(jnp.where(own == at, dense, 0.0)), pick.astype(jnp.bfloat16))


def reorder(values, seq, back=False):
    outer = (seq, 4) if back else (4, seq)
    cut = values.reshape(values.shape[0], *outer, values.shape[1] // (4 * seq))
    return cut.transpose(0, 2, 1, 3).reshape(values.shape)


def shards(
    tokens,
    doc_lengths,
    out_grad,
    mix_gain,
    branch_weight,
    input_weight,
    branch_bias,
    input_bias,
    conv_taps,
    conv_bias,
    rate_weight,
    entry_weight,
    rate_bias,
    entry_bias,
    decay_param,
    out_weight,
    out_bias,
    mlp_gain,
    gate_weight,
    up_weight,
    down_weight,
):
    z_count = lax.axis_size("z")
    seq = 2 * z_count
    s = 2 * lax.axis_index("z") + here_x()
    rows, model = tokens.shape[1:]
    block_w = rate_weight.shape[1]
    tap_count = conv_taps.shape[1]
    width = branch_weight.shape[1] // 8
    full_w = -(-width // 128) * 128
    hidden_w = gate_weight.shape[1] // 8
    heads = width // block_w
    own_r = conv_bias.shape[0]
    own_d = mix_gain.shape[0]
    groups, blocks = 4, 8
    every = blocks * rows

    pack_w = -(-(2 * block_w + tap_count + 6) // 128) * 128
    lengths = jnp.concatenate([doc_lengths] + [across_batch(doc_lengths, k) for k in (2, 1, 3)], 0)
    model_vec = jnp.stack([mix_gain, mlp_gain, out_bias], axis=1)
    model_vec = jnp.pad(model_vec, ((0, 0), (0, 125)))
    rec_cut = cut([branch_weight, out_weight, input_weight], full_w, model_vec)
    weight_rows = 8 * own_d
    rec_rows = swap_eight(rec_cut).reshape(weight_rows, -1)

    own_tokens = reorder(after(tokens[0], rec_cut), seq)
    vectors = jnp.stack(
        [branch_bias, input_bias, conv_bias, rate_bias, entry_bias, decay_param], axis=1
    )
    pack = jnp.concatenate([after(rate_weight, rec_cut), entry_weight, conv_taps, vectors], axis=1)
    pack = jnp.pad(pack, ((0, 0), (0, pack_w - pack.shape[1])))
    pack = jnp.concatenate(in_x_order(pack, flip_x(pack)), axis=0)
    first = gather_z_now(jnp.concatenate([rec_rows[:, 2 * full_w :], pack], axis=0))
    tokens_parts, _, tokens_last = gather_eight(after(own_tokens, rec_rows, lengths))
    first = in_z_order(after(first, tokens_last))

    input_all = first[:, :weight_rows].reshape(model, full_w)
    pack_all = first[:, weight_rows:].reshape(-1, pack_w)
    model_full = wide(input_all[:, width : width + 3]).T
    mix_scale, mlp_scale, out_b = model_full[0], model_full[1], model_full[2]
    rec_full = gather_z(after(rec_rows[:, : 2 * full_w], tokens_last))
    branch_full, out_full = rec_full[:, :full_w], rec_full[:, full_w:]

    mlp_cut = cut(after((gate_weight, up_weight, down_weight), rec_rows), hidden_w)
    mlp_sent = after(mlp_cut, tokens_last)
    grad_low = reorder(after(out_grad[0], rec_rows), seq)

    by_channel = lax.dynamic_slice_in_dim(pack_all, here_x() * width, width, 0)
    by_channel = jnp.pad(by_channel, ((0, full_w - width), (0, 0)))
    rate_dense = head_diagonal(by_channel[:, :block_w], heads, block_w)
    entry_dense = head_diagonal(by_channel[:, block_w : 2 * block_w], heads, block_w)
    channel_vec = wide(by_channel[:, 2 * block_w : 2 * block_w + tap_count + 6]).T
    tap_vals = channel_vec[:tap_count]
    branch_b, input_b, conv_b, rate_b, entry_b, decay_full = [
        channel_vec[tap_count + i] for i in range(6)
    ]
    layouts = [doc_layout(lengths, place * rows, rows + tap_count - 1) for place in (s, s ^ 1)]
    places, start_mask, begins = [
        jnp.stack([one, other], axis=1).reshape(blocks, -1) for one, other in zip(*layouts)
    ]
    own_start = start_mask[:, :rows, None]
    keep_mask = 1.0 - own_start.astype(jnp.float32)

    normed_low = [low(wide(part) * inv_root(wide(part)) * mix_scale) for part in tokens_parts]
    normed_low = lax.optimization_barrier(jnp.concatenate(normed_low, axis=0))
    own_channel = jnp.arange(full_w) < width
    input_full = jnp.where(own_channel, input_all, jnp.zeros((), jnp.bfloat16))
    conv_in = low(plain_dot(normed_low, input_full) + input_b).reshape(groups, 2, rows, full_w)
    mlp_rows = swap_eight(mlp_sent, conv_in).reshape(weight_rows, -1)
    gate_full = gather_z(mlp_rows[:, :hidden_w])
    up_full = gather_z(mlp_rows[:, hidden_w : 2 * hidden_w])
    down_full = gather_z(mlp_rows[:, 2 * hidden_w :])
    two_full = jnp.concatenate([gate_full, up_full], axis=1)
    x = here_x()

    def rims(values, first, last, hops):
        edge = values[:, :, first:last]
        forward = hops[0][1] > hops[0][0]
        sent_block, near_block = in_x_order(edge[:, 0], edge[:, 1])
        if forward:
            sent_block, near_block = near_block, sent_block
        got = along_z(sent_block, hops)
        at_edge = x == 0 if forward else x == 1
        own_rim = jnp.where(at_edge, got, edge[:, 1])
        other_rim = jnp.where(at_edge, edge[:, 0], got)
        return jnp.stack([own_rim, other_rim], axis=1)

    before = rims(conv_in, rows - RIM, rows, [(i, i + 1) for i in range(z_count - 1)])
    conv_in = jnp.concatenate([before, conv_in], axis=2).reshape(blocks, RIM + rows, full_w)

    def behind(offset):
        return conv_in[:, RIM - offset : RIM - offset + rows]

    def valid(offset, ahead):
        at = slice(offset, offset + rows) if ahead else slice(0, rows)
        return wide(places[:, at] - offset >= begins[:, at])[:, :, None]

    conv_val = jnp.zeros((blocks, rows, full_w), jnp.float32) + conv_b
    for offset in range(tap_count):
        conv_val = conv_val + tap_vals[offset] * wide(behind(offset)) * valid(offset, False)
    conv_low = low(conv_val)
    conv_flat = after(conv_low, rec_full).reshape(every, full_w)
    rate_pre = (plain_dot(conv_flat, rate_dense) + rate_b).reshape(blocks, rows, full_w)
    entry_pre = (plain_dot(conv_flat, entry_dense) + entry_b).reshape(blocks, rows, full_w)

    def gate_piece(rate_in, entry_in, conv_part, decay_in):
        return lru_gates(rate_in, entry_in, conv_part, decay_in, keep_mask, own_start)

    (decay_a, drive), gate_pull = jax.vjp(gate_piece, rate_pre, entry_pre, wide(conv_low), decay_full)
    cum_decay, local_state = local_scan(after(decay_a, mlp_rows), drive, False)
    grad_parts, _, grad_last = gather_eight(after(grad_low, mlp_rows), cum_decay)
    grad_all = jnp.concatenate(grad_parts, axis=0)
    carry_in = carried_in(
        cum_decay[:, -1].reshape(groups, 2, full_w), local_state[:, -1].reshape(groups, 2, full_w), False
    ).reshape(blocks, full_w)
    hidden = local_state + cum_decay * carry_in[:, None]
    branch_pre = plain_dot(normed_low, branch_full) + branch_b
    branch_val, branch_pull = jax.vjp(gelu_tanh, branch_pre)
    merged = after(low(hidden.reshape(every, full_w) * branch_val), gate_full, grad_last)

    def token_terms(part, weight):
        return low(against_rows(part, weight)).reshape(4, rows, model)

    def eight_terms(values, weight):
        theirs = token_terms(values[every // 2 :], weight)
        return token_terms(values[: every // 2], weight), theirs

    inputs = wide(own_tokens)
    mine, theirs = eight_terms(merged, out_full)
    got = scatter_first(theirs)
    ways = after(scatter_diagonal(mine, got), grad_parts)
    last = after(scatter_last(mine, got, ways), up_full, grad_all)
    residual = inputs + scatter_sum(mine, got, last) + out_b
    scale_two = inv_root(residual)
    normed_two = low(residual * scale_two * mlp_scale)
    normed_two_all = jnp.concatenate(gather_eight(normed_two)[0], axis=0)

    activated, placed, two_grad = mlp(after(normed_two_all, down_full), grad_all, two_full, down_full, rows)
    theirs = token_terms(two_grad[every // 2 :], two_full)
    got = scatter_first(theirs)
    block_part = low(against_rows(after(placed, theirs), down_full))
    block_sum = lax.psum_scatter(block_part, ("batch", "x"), scatter_dimension=0, tiled=True)
    mine = token_terms(after(two_grad, block_part)[: every // 2], two_full)
    down_term = low(outer_sum(grad_all, activated))
    ways = after(scatter_diagonal(mine, got), down_term)
    last = scatter_last(mine, got, ways)
    two_term = low(outer_sum(normed_two_all, two_grad))
    down_share = scatter_z(down_term)
    two_share = scatter_z(two_term)
    last = after(last, two_term, block_sum)
    normed_two_grad = scatter_sum(mine, got, last)
    residual_part, mlp_gain_term = norm_backward(residual, scale_two, mlp_scale, normed_two_grad)
    residual_grad = wide(grad_low) + residual_part
    mix_low = low(residual_grad)
    out_bias_term = jnp.sum(wide(mix_low), axis=0)
    mix_all = jnp.concatenate(gather_eight(mix_low)[0], axis=0)

    merged_grad = plain_dot(after(mix_all, down_share), out_full)
    state_grad = (merged_grad * branch_val).reshape(blocks, rows, full_w)
    next_decay = jnp.concatenate([decay_a[:, 1:], jnp.ones((blocks, 1, full_w), jnp.float32)], axis=1)
    cum_back, local_adjoint = local_scan(next_decay, state_grad, True)
    first_decay = decay_a[:, 0]
    adjoint_in = carried_in(
        (first_decay * cum_back[:, 0]).reshape(groups, 2, full_w),
        (first_decay * local_adjoint[:, 0]).reshape(groups, 2, full_w),
        True,
    ).reshape(blocks, full_w)
    branch_low = low(branch_pull(merged_grad * hidden.reshape(every, full_w))[0])
    out_term = low(outer_sum(mix_all, merged))
    branch_term = outer_sum(normed_low, branch_low)
    rec_term = jnp.concatenate([out_term, low(branch_term)], axis=1)
    rec_share = scatter_z(rec_term)
    adjoint = local_adjoint + cum_back * after(adjoint_in, rec_term)[:, None]
    prev_state = jnp.concatenate([carry_in[:, None], hidden[:, :-1]], axis=1)
    rate_grad, entry_grad, conv_direct, decay_term = gate_pull((adjoint * prev_state, adjoint))
    rate_low = low(rate_grad).reshape(every, full_w)
    entry_low = low(entry_grad).reshape(every, full_w)
    conv_grad = (
        conv_direct.reshape(every, full_w)
        + against_rows(rate_low, rate_dense)
        + against_rows(entry_low, entry_dense)
    )
    conv_grad_low = low(conv_grad).reshape(groups, 2, rows, full_w)
    after_rim = rims(conv_grad_low, 0, RIM, [(i + 1, i) for i in range(z_count - 1)])
    grad_ext = wide(jnp.concatenate([conv_grad_low, after_rim[:, :, : tap_count - 1]], axis=2))
    grad_ext = grad_ext.reshape(blocks, rows + tap_count - 1, full_w)
    conv_grad_f = wide(conv_grad_low).reshape(blocks, rows, full_w)
    input_grad = jnp.zeros((blocks, rows, full_w), jnp.float32)
    for offset in range(tap_count):
        input_grad = (
            input_grad
            + tap_vals[offset] * grad_ext[:, offset : offset + rows] * valid(offset, True)
        )
    input_low = low(input_grad).reshape(every, full_w)
    both_low = jnp.concatenate([branch_low, input_low], axis=1)
    both_full = jnp.concatenate([branch_full, input_full], axis=1)
    mix_theirs = token_terms(both_low[every // 2 :], both_full)
    mix_mine = token_terms(both_low[: every // 2], both_full)
    got = scatter_first(mix_theirs)
    ways = scatter_diagonal(mix_mine, got)

    block_out = reorder(low(residual + wide(block_sum)), seq, True)
    input_low, branch_sum = after((input_low, branch_low), mix_mine, mix_theirs)
    input_term = outer_sum(normed_low, input_low)
    conv_grad_f, rate_low, entry_low = after((conv_grad_f, rate_low, entry_low), mix_mine, mix_theirs)
    tap_terms = [
        jnp.sum(conv_grad_f * valid(offset, False) * wide(behind(offset)), axis=(0, 1))
        for offset in range(tap_count)
    ]
    mix_gain_term = branch_term * wide(branch_full) + input_term * wide(input_full)
    mix_gain_term = jnp.sum(mix_gain_term, axis=1) / mix_scale
    model_terms = jnp.stack([mix_gain_term, mlp_gain_term, out_bias_term], axis=1)
    model_terms = jnp.pad(model_terms, ((0, 0), (0, full_w - width - 3)))
    input_block = low(jnp.concatenate([input_term[:, :width], model_terms], axis=1))

    rate_term = head_blocks(outer_sum(conv_flat, rate_low), block_w)
    entry_term = head_blocks(outer_sum(conv_flat, entry_low), block_w)

    def column_sum(values):
        return jnp.sum(wide(values), axis=0)

    channel_terms = jnp.stack(
        tap_terms
        + [
            column_sum(branch_sum),
            column_sum(input_low),
            jnp.sum(conv_grad_f, axis=(0, 1)),
            column_sum(rate_low),
            column_sum(entry_low),
            decay_term,
        ],
        axis=1,
    )
    small = low(jnp.concatenate([rate_term, entry_term, channel_terms], axis=1))[:width]
    small = jnp.pad(small, ((0, 0), (0, pack_w - small.shape[1])))
    small = lax.dynamic_update_slice_in_dim(
        jnp.zeros((2 * width, pack_w), jnp.bfloat16), small, x * width, 0
    )
    input_block = jnp.concatenate(
        [input_block.reshape(z_count, weight_rows, -1), small.reshape(z_count, 2 * own_r, -1)], axis=1
    ).reshape(-1, pack_w)
    input_share = scatter_z(after(input_block, rec_share))
    ways = after(ways, two_share)
    last = after(scatter_last(mix_mine, got, ways), input_block)
    normed_grad = scatter_sum(mix_mine, got, last)
    mlp_share = jnp.concatenate([two_share, down_share], axis=1)
    two_back = swap_eight(after(mlp_share, normed_grad).reshape(8, own_d, -1), joined=3)
    input_part, _ = norm_backward(inputs, inv_root(inputs), mix_scale, normed_grad)
    tokens_grad = reorder(residual_grad + input_part, seq, True)[None]
    rec_back = swap_eight(
        jnp.concatenate([rec_share, input_share[:weight_rows]], axis=1).reshape(8, own_d, -1),
        normed_grad,
    )
    small_share = after(input_share[weight_rows:], normed_grad).reshape(2, own_r, pack_w)
    channel_sum = wide(lax.dynamic_index_in_dim(small_share, x, 0, False)) + wide(
        flip_x(lax.dynamic_index_in_dim(small_share, 1 - x, 0, False))
    )
    vec_sum = channel_sum[:, 2 * block_w :]
    model_at = 2 * full_w + width
    model_out = jnp.sum(wide(rec_back[:, :, model_at : model_at + 3]), axis=0)
    at = tap_count
    return (
        block_out[None],
        tokens_grad,
        model_out[:, 0],
        whole_rows(rec_back, full_w, full_w + width),
        whole_rows(rec_back, 2 * full_w, 2 * full_w + width),
        vec_sum[:, at],
        vec_sum[:, at + 1],
        vec_sum[:, :tap_count],
        vec_sum[:, at + 2],
        channel_sum[:, :block_w],
        channel_sum[:, block_w : 2 * block_w],
        vec_sum[:, at + 3],
        vec_sum[:, at + 4],
        vec_sum[:, at + 5],
        whole_rows(rec_back, 0, width),
        model_out[:, 2],
        model_out[:, 1],
        *two_back,
    )


def solution(mesh):
    batch, seq = mesh.shape["batch"], mesh.shape["seq"]
    fine = Mesh(mesh.devices.reshape(batch, seq // 2, 2), ("batch", "z", "x"))
    everywhere = ("batch", "z", "x")
    vector, matrix = P(everywhere), P(everywhere, None)
    block = P("batch", ("z", "x"), None)
    weights = (
        vector,
        matrix,
        matrix,
        vector,
        vector,
        matrix,
        vector,
        matrix,
        matrix,
        vector,
        vector,
        vector,
        matrix,
        vector,
        vector,
        matrix,
        matrix,
        matrix,
    )
    return jax.shard_map(
        shards,
        mesh=fine,
        in_specs=(block, P("batch", None), block) + weights,
        out_specs=(block, block) + weights,
        check_vma=False,
    )
```

```python
import functools

import jax
import jax.numpy as jnp
from jax import lax
from jax.experimental import pallas as pl
from jax.experimental.pallas import tpu as pltpu
from jax.sharding import Mesh
from jax.sharding import PartitionSpec as P

RIM = 16


def plain_dot(first_op, second_op):
    return jnp.dot(first_op, second_op, preferred_element_type=jnp.float32)


def outer_sum(first_op, second_op):
    return lax.dot_general(
        first_op, second_op, (((0,), (0,)), ((), ())), preferred_element_type=jnp.float32
    )


def against_rows(first_op, second_op):
    return lax.dot_general(
        first_op, second_op, (((1,), (1,)), ((), ())), preferred_element_type=jnp.float32
    )


def gelu_tanh(values):
    return jax.nn.gelu(values, approximate=True)


def low(values):
    return values.astype(jnp.bfloat16)


def wide(values):
    return values.astype(jnp.float32)


def across_batch(block, flip):
    return lax.ppermute(block, "batch", [(i, i ^ flip) for i in range(lax.axis_size("batch"))])


def flip_x(block):
    return lax.ppermute(block, "x", [(0, 1), (1, 0)])


def along_z(block, hops):
    return lax.ppermute(block, "z", hops)


def flip_z(block, by):
    return along_z(block, [(i, i ^ by) for i in range(lax.axis_size("z"))])


def after(value, *others):
    return lax.optimization_barrier((value, *others))[0]


def here_x():
    return lax.axis_index("x")


def in_x_order(mine, other):
    first = here_x() == 0
    return [jnp.where(first, mine, other), jnp.where(first, other, mine)]


def across(block, flip_b, flip_xs):
    if flip_b == 0 and flip_xs == 0:
        return block
    places = range(2 * lax.axis_size("batch"))
    return lax.ppermute(block, ("batch", "x"), [(i, i ^ (2 * flip_b + flip_xs)) for i in places])


EIGHT = [(k, j) for j in range(2) for k in (2, 1, 3, 0)]


def place_kernel(place_of, *refs):
    out_ref = refs[-1]
    for i, ref in enumerate(refs[:-1]):
        out_ref[place_of(i)] = ref[...]


def place(parts, place_of):
    return pl.pallas_call(
        functools.partial(place_kernel, place_of),
        out_shape=jax.ShapeDtypeStruct((len(parts),) + parts[0].shape, parts[0].dtype),
        compiler_params=pltpu.CompilerParams(vmem_limit_bytes=32 * 2**20),
        cost_estimate=pl.CostEstimate(
            flops=0, bytes_accessed=4 * len(parts) * parts[0].size, transcendentals=0
        ),
    )(*parts)


def join_kernel(count, place_of, *refs):
    ins, outs = refs[:-count], refs[-count:]
    width = ins[0].shape[1] // count
    for i, ref in enumerate(ins):
        place = place_of(i)
        first = pl.multiple_of((place % 4 * 2 + place // 4) * width, 128)
        for n, out in enumerate(outs):
            out[:, pl.ds(first, width)] = ref[:, n * width : (n + 1) * width].astype(jnp.float32)


def join(parts, place_of, count):
    rows, width = parts[0].shape
    shape = jax.ShapeDtypeStruct((rows, 8 * width // count), jnp.float32)
    return pl.pallas_call(
        functools.partial(join_kernel, count, place_of),
        out_shape=[shape] * count,
        compiler_params=pltpu.CompilerParams(vmem_limit_bytes=32 * 2**20),
        cost_estimate=pl.CostEstimate(
            flops=0, bytes_accessed=48 * rows * width, transcendentals=0
        ),
    )(*parts)


def swap_eight(blocks, *meanwhile, joined=0):
    x, b = here_x(), lax.axis_index("batch")
    got = []
    for k, j in EIGHT:
        block = lax.dynamic_index_in_dim(blocks, (x ^ j) * 4 + (b ^ k), 0, False)
        got.append(across(block, k, j))

    def place_of(i):
        k, j = EIGHT[i]
        return (here_x() ^ j) * 4 + (lax.axis_index("batch") ^ k)

    got = after(got, *meanwhile)
    return join(got, place_of, joined) if joined else place(got, place_of)


def gather_eight(block, *meanwhile):
    half = block.shape[0] // 2
    over_y = across_batch(block, 2)
    over_x = flip_x(block)
    over_y, over_x = after((over_y, over_x), *meanwhile)
    both_a = flip_x(over_y[:half])
    both_b = across_batch(over_x[half:], 2)
    here = [block, over_x, over_y, both_a, both_b]
    return here + [across_batch(part, 1) for part in here], over_y, (both_a, both_b)


def scatter_first(theirs):
    return [across_batch(theirs[k], 1) for k in range(4)]


def scatter_diagonal(mine, got):
    both = wide(mine[3]) + wide(got[3])
    half = both.shape[0] // 2
    return flip_x(low(both[:half])), across_batch(low(both[half:]), 2)


def scatter_last(mine, got, ways):
    mine, got = after((mine, got), ways)
    over_x, over_y = wide(mine[1]) + wide(got[1]), wide(mine[2]) + wide(got[2])
    half = over_x.shape[0] // 2
    over_y = jnp.concatenate([over_y[:half] + wide(ways[0]), over_y[half:]], axis=0)
    over_x = jnp.concatenate([over_x[:half], over_x[half:] + wide(ways[1])], axis=0)
    return across_batch(low(over_y), 2), flip_x(low(over_x))


def scatter_sum(mine, got, last):
    mine, got = after((mine[0], got[0]), last)
    return wide(mine) + wide(got) + wide(last[0]) + wide(last[1])


def gather_z(block):
    return lax.all_gather(block, "z", axis=0, tiled=True)


def scatter_z(term):
    return lax.psum_scatter(term, "z", scatter_dimension=0, tiled=True)


def cut_kernel(width, full, extra, *refs):
    out_ref = refs[-1]
    ins = refs[:-1]
    rows = out_ref.shape[1]
    for i in range(out_ref.shape[0]):
        first = (i % 4 * 2 + i // 4) * width
        pieces = []
        for n, ref in enumerate(ins[: len(ins) - extra]):
            piece = ref[:, first : first + width]
            if full > width:
                tail = jnp.zeros((rows, full - width), piece.dtype)
                if extra and n == len(ins) - extra - 1:
                    tail = ins[-1][:, : full - width]
                piece = jnp.concatenate([piece, tail], axis=1)
            pieces.append(piece)
        out_ref[i] = jnp.concatenate(pieces, axis=1)


def cut(weights, full, common=None):
    rows = weights[0].shape[0]
    ins = list(weights) + ([] if common is None else [common])
    return pl.pallas_call(
        functools.partial(cut_kernel, weights[0].shape[1] // 8, full, 0 if common is None else 1),
        out_shape=jax.ShapeDtypeStruct((8, rows, full * len(weights)), weights[0].dtype),
        compiler_params=pltpu.CompilerParams(vmem_limit_bytes=32 * 2**20),
        cost_estimate=pl.CostEstimate(
            flops=0, bytes_accessed=4 * weights[0].size * len(weights), transcendentals=0
        ),
    )(*ins)


def whole_rows(parts, first, last):
    return wide(
        jnp.concatenate([parts[i * 4 + j, :, first:last] for j in range(4) for i in range(2)], axis=1)
    )


def in_run_order(own, other, reverse):
    first, second = in_x_order(own, other)
    return (second, first) if reverse else (first, second)


def carried_in(decay, state, reverse):
    z = lax.axis_index("z")
    count = lax.axis_size("z")
    decay_one, decay_two = in_run_order(decay[:, 0], decay[:, 1], reverse)
    state_one, state_two = in_run_order(state[:, 0], state[:, 1], reverse)
    total_a, total_b = decay_one * decay_two, decay_two * state_one + state_two
    enter_a, enter_b = jnp.ones_like(total_a), jnp.zeros_like(total_b)
    bit = 1
    while bit < count:
        got = flip_z(jnp.stack([total_a, total_b]), bit)
        got_a, got_b = got[0], got[1]
        theirs_first = ((z & bit) == 0) if reverse else ((z & bit) != 0)
        enter_b = jnp.where(theirs_first, enter_a * got_b + enter_b, enter_b)
        enter_a = jnp.where(theirs_first, enter_a * got_a, enter_a)
        total_b = jnp.where(theirs_first, total_a * got_b + total_b, got_a * total_b + got_b)
        total_a = total_a * got_a
        bit *= 2
    second = decay_one * enter_b + state_one
    return jnp.stack(in_run_order(enter_b, second, reverse), axis=1)


def scan_kernel(reverse, a_ref, b_ref, cum_ref, out_ref):
    groups, rows, lanes = a_ref.shape
    tiles = rows // 8
    row = lax.broadcasted_iota(jnp.int32, (8, lanes), 0)

    def step(i, carry):
        tile = tiles - 1 - i if reverse else i
        at = pl.ds(pl.multiple_of(tile * 8, 8), 8)
        after = []
        for g in range(groups):
            a, b = a_ref[g, at, :], b_ref[g, at, :]
            for shift in (1, 2, 4):
                by = 8 - shift if reverse else shift
                ok = row < 8 - shift if reverse else row >= shift
                a_far = jnp.where(ok, pltpu.roll(a, by, 0), 1.0)
                b_far = jnp.where(ok, pltpu.roll(b, by, 0), 0.0)
                b = b + a * b_far
                a = a * a_far
            cum, state = carry[g]
            b = b + a * state
            a = a * cum
            cum_ref[g, at, :] = a
            out_ref[g, at, :] = b
            last = 0 if reverse else 7
            after.append(
                (
                    jnp.broadcast_to(a[last : last + 1], (8, lanes)),
                    jnp.broadcast_to(b[last : last + 1], (8, lanes)),
                )
            )
        return tuple(after)

    start = tuple(
        (jnp.ones((8, lanes), jnp.float32), jnp.zeros((8, lanes), jnp.float32))
        for _ in range(groups)
    )
    lax.fori_loop(0, tiles, step, start)


def local_scan(decay, drive, reverse):
    groups, rows, width = decay.shape
    lanes = 128 if width % 128 == 0 else width
    spec = pl.BlockSpec((groups, rows, lanes), lambda i: (0, 0, i))
    shape = jax.ShapeDtypeStruct(decay.shape, jnp.float32)
    return pl.pallas_call(
        functools.partial(scan_kernel, reverse),
        grid=(width // lanes,),
        in_specs=[spec, spec],
        out_specs=[spec, spec],
        out_shape=[shape, shape],
        cost_estimate=pl.CostEstimate(
            flops=20 * decay.size, bytes_accessed=16 * decay.size, transcendentals=0
        ),
    )(decay, drive)


def mlp_kernel(normed_ref, grad_ref, two_ref, down_ref, act_ref, out_ref):
    width = act_ref.shape[1]
    lane = 256 if width % 256 == 0 else width
    normed, grad = normed_ref[...], grad_ref[...]
    for first in range(0, width, lane):
        at, up_at = slice(first, first + lane), slice(width + first, width + first + lane)
        gate = plain_dot(normed, two_ref[:, at])
        up = plain_dot(normed, two_ref[:, up_at])
        act_grad = plain_dot(grad, down_ref[:, at])
        square = gate * gate
        slope = 0.7978845608028654
        bent = jnp.tanh(slope * gate * (1.0 + 0.044715 * square))
        half = 0.5 + 0.5 * bent
        act = half * gate
        act_slope = half + 0.5 * gate * (1.0 - bent * bent) * (slope * (1.0 + 0.134145 * square))
        act_ref[:, at] = low(act * up)
        out_ref[:, at] = low(act_grad * up * act_slope)
        out_ref[:, up_at] = low(act_grad * act)


def mlp(normed, grad, two_full, down_full, rows):
    count, model = normed.shape
    width = down_full.shape[1]

    def block(columns):
        return pl.BlockSpec((rows, columns), lambda i: (i, 0))

    def whole(columns):
        return pl.BlockSpec((model, columns), lambda i: (0, 0))

    return pl.pallas_call(
        mlp_kernel,
        grid=(count // rows,),
        in_specs=[block(model), block(model), whole(2 * width), whole(width)],
        out_specs=[block(width), block(2 * width)],
        out_shape=[
            jax.ShapeDtypeStruct((count, width), jnp.bfloat16),
            jax.ShapeDtypeStruct((count, 2 * width), jnp.bfloat16),
        ],
        compiler_params=pltpu.CompilerParams(vmem_limit_bytes=56 * 2**20),
        cost_estimate=pl.CostEstimate(
            flops=6 * count * model * width,
            bytes_accessed=2 * (2 * count * model + 3 * model * width + 4 * count * width),
            transcendentals=count * width,
        ),
    )(normed, grad, two_full, down_full)


def doc_layout(lengths, first_pos, span_count):
    second = lengths[:, 0:1]
    third = second + lengths[:, 1:2]
    places = first_pos + lax.broadcasted_iota(jnp.int32, (lengths.shape[0], span_count), 1)
    begins = jnp.where(places >= third, third, jnp.where(places >= second, second, 0))
    return places, places == begins, begins


def lru_gates(rate_in, entry_in, conv_in, decay_in, keep_mask, start_mask):
    rate_sig = jax.nn.sigmoid(rate_in)
    entry_sig = jax.nn.sigmoid(entry_in)
    log_decay = -8.0 * rate_sig * jax.nn.softplus(-decay_in)
    drive_scale = jnp.where(start_mask, 1.0, jnp.sqrt(-jnp.expm1(2.0 * log_decay)))
    return (jnp.exp(log_decay) * keep_mask, drive_scale * entry_sig * conv_in)


def inv_root(values):
    return lax.rsqrt(jnp.mean(values * values, axis=-1, keepdims=True) + 1e-06)


def norm_backward(values, scale, gain_vec, incoming):
    weighted = incoming * gain_vec
    inner_mean = jnp.mean(weighted * values, axis=-1, keepdims=True)
    return (
        scale * weighted - values * scale * scale * scale * inner_mean,
        jnp.sum(incoming * values * scale, axis=0),
    )


def head_diagonal(blocks, heads, width):
    size = blocks.shape[0]
    own = lax.broadcasted_iota(jnp.int32, (size, size), 0) // width
    at = lax.broadcasted_iota(jnp.int32, (size, size), 1) // width
    copies = jnp.tile(blocks, (1, heads))
    copies = jnp.pad(copies, ((0, 0), (0, size - heads * width)))
    return jnp.where(own == at, copies, jnp.zeros((), blocks.dtype))


def head_blocks(dense, width):
    size = dense.shape[0]
    own = lax.broadcasted_iota(jnp.int32, (size, size), 0) // width
    at = lax.broadcasted_iota(jnp.int32, (size, size), 1) // width
    pick = lax.broadcasted_iota(jnp.int32, (size, width), 0) % width
    pick = pick == lax.broadcasted_iota(jnp.int32, (size, width), 1)
    return plain_dot(low(jnp.where(own == at, dense, 0.0)), pick.astype(jnp.bfloat16))


def reorder_kernel(chunks, in_ref, out_ref):
    width = in_ref.shape[1] // len(chunks)
    for first in range(0, len(chunks), 2):
        pair = [in_ref[:, c * width : (c + 1) * width] for c in chunks[first : first + 2]]
        out_ref[:, first * width : (first + 2) * width] = jnp.concatenate(pair, axis=1)


def reorder(values, seq, back=False):
    outer = (seq, 4) if back else (4, seq)
    width = values.shape[1] // (4 * seq)
    if width == 64:
        chunks = [j * outer[1] + i for i in range(outer[1]) for j in range(outer[0])]
        return pl.pallas_call(
            functools.partial(reorder_kernel, chunks),
            out_shape=jax.ShapeDtypeStruct(values.shape, values.dtype),
            compiler_params=pltpu.CompilerParams(vmem_limit_bytes=32 * 2**20),
            cost_estimate=pl.CostEstimate(
                flops=0, bytes_accessed=8 * values.size, transcendentals=0
            ),
        )(values)
    cut = values.reshape(values.shape[0], *outer, width)
    return cut.transpose(0, 2, 1, 3).reshape(values.shape)


def shards(
    tokens,
    doc_lengths,
    out_grad,
    mix_gain,
    branch_weight,
    input_weight,
    branch_bias,
    input_bias,
    conv_taps,
    conv_bias,
    rate_weight,
    entry_weight,
    rate_bias,
    entry_bias,
    decay_param,
    out_weight,
    out_bias,
    mlp_gain,
    gate_weight,
    up_weight,
    down_weight,
):
    z_count = lax.axis_size("z")
    seq = 2 * z_count
    s = 2 * lax.axis_index("z") + here_x()
    rows, model = tokens.shape[1:]
    block_w = rate_weight.shape[1]
    tap_count = conv_taps.shape[1]
    width = branch_weight.shape[1] // 8
    full_w = -(-width // 128) * 128
    hidden_w = gate_weight.shape[1] // 8
    heads = width // block_w
    own_r = conv_bias.shape[0]
    own_d = mix_gain.shape[0]
    groups, blocks = 4, 8
    every = blocks * rows

    pack_w = -(-(2 * block_w + tap_count + 6) // 128) * 128
    lengths = jnp.concatenate([doc_lengths] + [across_batch(doc_lengths, k) for k in (2, 1, 3)], 0)
    model_vec = jnp.stack([mix_gain, mlp_gain, out_bias], axis=1)
    model_vec = jnp.pad(model_vec, ((0, 0), (0, 125)))
    rec_cut = cut([branch_weight, out_weight, input_weight], full_w, model_vec)
    weight_rows = 8 * own_d
    rec_rows = swap_eight(rec_cut).reshape(weight_rows, -1)

    own_tokens = reorder(after(tokens[0], rec_cut), seq)
    vectors = jnp.stack(
        [branch_bias, input_bias, conv_bias, rate_bias, entry_bias, decay_param], axis=1
    )
    pack = jnp.concatenate([after(rate_weight, rec_cut), entry_weight, conv_taps, vectors], axis=1)
    pack = jnp.pad(pack, ((0, 0), (0, pack_w - pack.shape[1])))
    pack = jnp.concatenate(in_x_order(pack, flip_x(pack)), axis=0)
    first = gather_z(jnp.concatenate([rec_rows[:, 2 * full_w :], pack], axis=0)).reshape(z_count, -1, pack_w)
    tokens_parts, _, tokens_last = gather_eight(after(own_tokens, rec_rows, lengths))

    input_all = first[:, :weight_rows].reshape(model, full_w)
    pack_all = first[:, weight_rows:].reshape(-1, pack_w)
    model_full = wide(input_all[:, width : width + 3]).T
    mix_scale, mlp_scale, out_b = model_full[0], model_full[1], model_full[2]
    rec_full = gather_z(rec_rows[:, : 2 * full_w])
    branch_full, out_full = rec_full[:, :full_w], rec_full[:, full_w:]

    mlp_cut = cut(after((gate_weight, up_weight, down_weight), rec_rows), hidden_w)
    mlp_sent = after(mlp_cut, tokens_last)
    grad_low = reorder(after(out_grad[0], rec_rows), seq)

    by_channel = lax.dynamic_slice_in_dim(pack_all, here_x() * width, width, 0)
    by_channel = jnp.pad(by_channel, ((0, full_w - width), (0, 0)))
    rate_dense = head_diagonal(by_channel[:, :block_w], heads, block_w)
    entry_dense = head_diagonal(by_channel[:, block_w : 2 * block_w], heads, block_w)
    channel_vec = wide(by_channel[:, 2 * block_w : 2 * block_w + tap_count + 6]).T
    tap_vals = channel_vec[:tap_count]
    branch_b, input_b, conv_b, rate_b, entry_b, decay_full = [
        channel_vec[tap_count + i] for i in range(6)
    ]
    layouts = [doc_layout(lengths, place * rows, rows + tap_count - 1) for place in (s, s ^ 1)]
    places, start_mask, begins = [
        jnp.stack([one, other], axis=1).reshape(blocks, -1) for one, other in zip(*layouts)
    ]
    own_start = start_mask[:, :rows, None]
    keep_mask = 1.0 - own_start.astype(jnp.float32)

    normed_low = [low(wide(part) * inv_root(wide(part)) * mix_scale) for part in tokens_parts]
    normed_low = lax.optimization_barrier(jnp.concatenate(normed_low, axis=0))
    own_channel = jnp.arange(full_w) < width
    input_full = jnp.where(own_channel, input_all, jnp.zeros((), jnp.bfloat16))
    conv_in = low(plain_dot(normed_low, input_full) + input_b).reshape(groups, 2, rows, full_w)
    mlp_rows = swap_eight(mlp_sent, conv_in).reshape(weight_rows, -1)
    gate_full = gather_z(mlp_rows[:, :hidden_w])
    up_full = gather_z(mlp_rows[:, hidden_w : 2 * hidden_w])
    down_full = gather_z(mlp_rows[:, 2 * hidden_w :])
    two_full = jnp.concatenate([gate_full, up_full], axis=1)
    x = here_x()

    def rims(values, first, last, hops):
        edge = values[:, :, first:last]
        forward = hops[0][1] > hops[0][0]
        sent_block, near_block = in_x_order(edge[:, 0], edge[:, 1])
        if forward:
            sent_block, near_block = near_block, sent_block
        got = along_z(sent_block, hops)
        at_edge = x == 0 if forward else x == 1
        own_rim = jnp.where(at_edge, got, edge[:, 1])
        other_rim = jnp.where(at_edge, edge[:, 0], got)
        return jnp.stack([own_rim, other_rim], axis=1)

    before = rims(conv_in, rows - RIM, rows, [(i, i + 1) for i in range(z_count - 1)])
    conv_in = jnp.concatenate([before, conv_in], axis=2).reshape(blocks, RIM + rows, full_w)

    def behind(offset):
        return conv_in[:, RIM - offset : RIM - offset + rows]

    def valid(offset, ahead):
        at = slice(offset, offset + rows) if ahead else slice(0, rows)
        return wide(places[:, at] - offset >= begins[:, at])[:, :, None]

    conv_val = jnp.zeros((blocks, rows, full_w), jnp.float32) + conv_b
    for offset in range(tap_count):
        conv_val = conv_val + tap_vals[offset] * wide(behind(offset)) * valid(offset, False)
    conv_low = low(conv_val)
    conv_flat = after(conv_low, rec_full).reshape(every, full_w)
    rate_pre = (plain_dot(conv_flat, rate_dense) + rate_b).reshape(blocks, rows, full_w)
    entry_pre = (plain_dot(conv_flat, entry_dense) + entry_b).reshape(blocks, rows, full_w)

    def gate_piece(rate_in, entry_in, conv_part, decay_in):
        return lru_gates(rate_in, entry_in, conv_part, decay_in, keep_mask, own_start)

    (decay_a, drive), gate_pull = jax.vjp(gate_piece, rate_pre, entry_pre, wide(conv_low), decay_full)
    cum_decay, local_state = local_scan(after(decay_a, mlp_rows), drive, False)
    grad_parts, _, grad_last = gather_eight(after(grad_low, mlp_rows), cum_decay)
    grad_all = jnp.concatenate(grad_parts, axis=0)
    carry_in = carried_in(
        cum_decay[:, -1].reshape(groups, 2, full_w), local_state[:, -1].reshape(groups, 2, full_w), False
    ).reshape(blocks, full_w)
    hidden = local_state + cum_decay * carry_in[:, None]
    branch_pre = plain_dot(normed_low, branch_full) + branch_b
    branch_val, branch_pull = jax.vjp(gelu_tanh, branch_pre)
    merged = after(low(hidden.reshape(every, full_w) * branch_val), gate_full, grad_last)

    def token_terms(part, weight):
        return low(against_rows(part, weight)).reshape(4, rows, model)

    def eight_terms(values, weight):
        theirs = token_terms(values[every // 2 :], weight)
        return token_terms(values[: every // 2], weight), theirs

    inputs = wide(own_tokens)
    mine, theirs = eight_terms(merged, out_full)
    got = scatter_first(theirs)
    ways = after(scatter_diagonal(mine, got), grad_parts)
    last = after(scatter_last(mine, got, ways), up_full, grad_all)
    residual = inputs + scatter_sum(mine, got, last) + out_b
    scale_two = inv_root(residual)
    normed_two = low(residual * scale_two * mlp_scale)
    normed_two_all = jnp.concatenate(gather_eight(normed_two)[0], axis=0)

    activated, two_grad = mlp(after(normed_two_all, down_full), grad_all, two_full, down_full, rows)
    theirs = token_terms(two_grad[every // 2 :], two_full)
    got = scatter_first(theirs)
    mine = token_terms(two_grad[: every // 2], two_full)
    down_term = low(outer_sum(grad_all, activated))
    ways = after(scatter_diagonal(mine, got), down_term)
    last = scatter_last(mine, got, ways)
    two_term = low(outer_sum(normed_two_all, two_grad))
    down_share = scatter_z(down_term)
    two_share = scatter_z(two_term)
    last = after(last, two_term)
    normed_two_grad = scatter_sum(mine, got, last)
    residual_part, mlp_gain_term = norm_backward(residual, scale_two, mlp_scale, normed_two_grad)
    residual_grad = wide(grad_low) + residual_part
    mix_low = low(residual_grad)
    out_bias_term = jnp.sum(wide(mix_low), axis=0)
    block_mine, block_theirs = eight_terms(activated, down_full)
    mix_all = jnp.concatenate(gather_eight(mix_low, block_mine, block_theirs)[0], axis=0)

    merged_grad = plain_dot(after(mix_all, down_share), out_full)
    state_grad = (merged_grad * branch_val).reshape(blocks, rows, full_w)
    next_decay = jnp.concatenate([decay_a[:, 1:], jnp.ones((blocks, 1, full_w), jnp.float32)], axis=1)
    cum_back, local_adjoint = local_scan(next_decay, state_grad, True)
    first_decay = decay_a[:, 0]
    adjoint_in = carried_in(
        (first_decay * cum_back[:, 0]).reshape(groups, 2, full_w),
        (first_decay * local_adjoint[:, 0]).reshape(groups, 2, full_w),
        True,
    ).reshape(blocks, full_w)
    branch_low = low(branch_pull(merged_grad * hidden.reshape(every, full_w))[0])
    out_term = low(outer_sum(mix_all, merged))
    branch_term = outer_sum(normed_low, branch_low)
    rec_term = jnp.concatenate([out_term, low(branch_term)], axis=1)
    rec_share = scatter_z(rec_term)
    adjoint = local_adjoint + cum_back * after(adjoint_in, rec_term)[:, None]
    prev_state = jnp.concatenate([carry_in[:, None], hidden[:, :-1]], axis=1)
    rate_grad, entry_grad, conv_direct, decay_term = gate_pull((adjoint * prev_state, adjoint))
    rate_low = low(rate_grad).reshape(every, full_w)
    entry_low = low(entry_grad).reshape(every, full_w)
    conv_grad = (
        conv_direct.reshape(every, full_w)
        + against_rows(rate_low, rate_dense)
        + against_rows(entry_low, entry_dense)
    )
    conv_grad_low = low(conv_grad).reshape(groups, 2, rows, full_w)
    after_rim = rims(conv_grad_low, 0, RIM, [(i + 1, i) for i in range(z_count - 1)])
    grad_ext = wide(jnp.concatenate([conv_grad_low, after_rim[:, :, : tap_count - 1]], axis=2))
    grad_ext = grad_ext.reshape(blocks, rows + tap_count - 1, full_w)
    conv_grad_f = wide(conv_grad_low).reshape(blocks, rows, full_w)
    input_grad = jnp.zeros((blocks, rows, full_w), jnp.float32)
    for offset in range(tap_count):
        input_grad = (
            input_grad
            + tap_vals[offset] * grad_ext[:, offset : offset + rows] * valid(offset, True)
        )
    input_low = low(input_grad).reshape(every, full_w)
    both_low = jnp.concatenate([branch_low, input_low], axis=1)
    both_full = jnp.concatenate([branch_full, input_full], axis=1)
    mix_theirs = token_terms(both_low[every // 2 :], both_full)
    mix_mine = token_terms(both_low[: every // 2], both_full)
    got = scatter_first(mix_theirs)
    ways = scatter_diagonal(mix_mine, got)

    input_low, branch_sum = after((input_low, branch_low), mix_mine, mix_theirs)
    input_term = outer_sum(normed_low, input_low)
    conv_grad_f, rate_low, entry_low = after((conv_grad_f, rate_low, entry_low), mix_mine, mix_theirs)
    tap_terms = [
        jnp.sum(conv_grad_f * valid(offset, False) * wide(behind(offset)), axis=(0, 1))
        for offset in range(tap_count)
    ]
    mix_gain_term = branch_term * wide(branch_full) + input_term * wide(input_full)
    mix_gain_term = jnp.sum(mix_gain_term, axis=1) / mix_scale
    model_terms = jnp.stack([mix_gain_term, mlp_gain_term, out_bias_term], axis=1)
    model_terms = jnp.pad(model_terms, ((0, 0), (0, full_w - width - 3)))
    input_block = low(jnp.concatenate([input_term[:, :width], model_terms], axis=1))

    rate_term = head_blocks(outer_sum(conv_flat, rate_low), block_w)
    entry_term = head_blocks(outer_sum(conv_flat, entry_low), block_w)

    def column_sum(values):
        return jnp.sum(wide(values), axis=0)

    channel_terms = jnp.stack(
        tap_terms
        + [
            column_sum(branch_sum),
            column_sum(input_low),
            jnp.sum(conv_grad_f, axis=(0, 1)),
            column_sum(rate_low),
            column_sum(entry_low),
            decay_term,
        ],
        axis=1,
    )
    small = low(jnp.concatenate([rate_term, entry_term, channel_terms], axis=1))[:width]
    small = jnp.pad(small, ((0, 0), (0, pack_w - small.shape[1])))
    small = lax.dynamic_update_slice_in_dim(
        jnp.zeros((2 * width, pack_w), jnp.bfloat16), small, x * width, 0
    )
    input_block = jnp.concatenate(
        [input_block.reshape(z_count, weight_rows, -1), small.reshape(z_count, 2 * own_r, -1)], axis=1
    ).reshape(-1, pack_w)
    input_share = scatter_z(after(input_block, rec_share))
    ways = after(ways, two_share)
    block_got = scatter_first(block_theirs)
    block_ways = scatter_diagonal(block_mine, after(block_got, ways))
    last = after(scatter_last(mix_mine, got, ways), input_block)
    normed_grad = scatter_sum(mix_mine, got, last)
    block_last = scatter_last(block_mine, block_got, after(block_ways, last))
    block_out = reorder(low(residual + scatter_sum(block_mine, block_got, block_last)), seq, True)
    mlp_share = jnp.concatenate([two_share, down_share], axis=1)
    two_back = swap_eight(after(mlp_share, ways).reshape(8, own_d, -1), normed_grad, joined=3)
    input_part, _ = norm_backward(inputs, inv_root(inputs), mix_scale, normed_grad)
    tokens_grad = reorder(residual_grad + input_part, seq, True)[None]
    rec_back = swap_eight(
        jnp.concatenate([rec_share, input_share[:weight_rows]], axis=1).reshape(8, own_d, -1),
        normed_grad,
    )
    small_share = after(input_share[weight_rows:], normed_grad).reshape(2, own_r, pack_w)
    channel_sum = wide(lax.dynamic_index_in_dim(small_share, x, 0, False)) + wide(
        flip_x(lax.dynamic_index_in_dim(small_share, 1 - x, 0, False))
    )
    vec_sum = channel_sum[:, 2 * block_w :]
    model_at = 2 * full_w + width
    model_out = jnp.sum(wide(rec_back[:, :, model_at : model_at + 3]), axis=0)
    at = tap_count
    return (
        block_out[None],
        tokens_grad,
        model_out[:, 0],
        whole_rows(rec_back, full_w, full_w + width),
        whole_rows(rec_back, 2 * full_w, 2 * full_w + width),
        vec_sum[:, at],
        vec_sum[:, at + 1],
        vec_sum[:, :tap_count],
        vec_sum[:, at + 2],
        channel_sum[:, :block_w],
        channel_sum[:, block_w : 2 * block_w],
        vec_sum[:, at + 3],
        vec_sum[:, at + 4],
        vec_sum[:, at + 5],
        whole_rows(rec_back, 0, width),
        model_out[:, 2],
        model_out[:, 1],
        *two_back,
    )


def solution(mesh):
    batch, seq = mesh.shape["batch"], mesh.shape["seq"]
    fine = Mesh(mesh.devices.reshape(batch, seq // 2, 2), ("batch", "z", "x"))
    everywhere = ("batch", "z", "x")
    vector, matrix = P(everywhere), P(everywhere, None)
    block = P("batch", ("z", "x"), None)
    weights = (
        vector,
        matrix,
        matrix,
        vector,
        vector,
        matrix,
        vector,
        matrix,
        matrix,
        vector,
        vector,
        vector,
        matrix,
        vector,
        vector,
        matrix,
        matrix,
        matrix,
    )
    return jax.shard_map(
        shards,
        mesh=fine,
        in_specs=(block, P("batch", None), block) + weights,
        out_specs=(block, block) + weights,
        check_vma=False,
    )
```

```python
import functools

import jax
import jax.numpy as jnp
from jax import lax
from jax.experimental import pallas as pl
from jax.experimental.pallas import tpu as pltpu
from jax.sharding import Mesh
from jax.sharding import PartitionSpec as P

RIM = 16


def plain_dot(first_op, second_op):
    return jnp.dot(first_op, second_op, preferred_element_type=jnp.float32)


def outer_sum(first_op, second_op):
    return lax.dot_general(
        first_op, second_op, (((0,), (0,)), ((), ())), preferred_element_type=jnp.float32
    )


def against_rows(first_op, second_op):
    return lax.dot_general(
        first_op, second_op, (((1,), (1,)), ((), ())), preferred_element_type=jnp.float32
    )


def gelu_tanh(values):
    return jax.nn.gelu(values, approximate=True)


def low(values):
    return values.astype(jnp.bfloat16)


def wide(values):
    return values.astype(jnp.float32)


def across_batch(block, flip):
    return lax.ppermute(block, "batch", [(i, i ^ flip) for i in range(lax.axis_size("batch"))])


def flip_x(block):
    return lax.ppermute(block, "x", [(0, 1), (1, 0)])


def along_z(block, hops):
    return lax.ppermute(block, "z", hops)


def flip_z(block, by):
    return along_z(block, [(i, i ^ by) for i in range(lax.axis_size("z"))])


def after(value, *others):
    return lax.optimization_barrier((value, *others))[0]


def here_x():
    return lax.axis_index("x")


def in_x_order(mine, other):
    first = here_x() == 0
    return [jnp.where(first, mine, other), jnp.where(first, other, mine)]


def across(block, flip_b, flip_xs):
    if flip_b == 0 and flip_xs == 0:
        return block
    places = range(2 * lax.axis_size("batch"))
    return lax.ppermute(block, ("batch", "x"), [(i, i ^ (2 * flip_b + flip_xs)) for i in places])


EIGHT = [(k, j) for j in range(2) for k in (2, 1, 3, 0)]


def place_kernel(place_of, *refs):
    out_ref = refs[-1]
    for i, ref in enumerate(refs[:-1]):
        out_ref[place_of(i)] = ref[...]


def place(parts, place_of):
    return pl.pallas_call(
        functools.partial(place_kernel, place_of),
        out_shape=jax.ShapeDtypeStruct((len(parts),) + parts[0].shape, parts[0].dtype),
        compiler_params=pltpu.CompilerParams(vmem_limit_bytes=32 * 2**20),
        cost_estimate=pl.CostEstimate(
            flops=0, bytes_accessed=4 * len(parts) * parts[0].size, transcendentals=0
        ),
    )(*parts)


def join_kernel(count, width, place_of, *refs):
    ins, outs, rest_ref = refs[: -count - 1], refs[-count - 1 : -1], refs[-1]
    for i, ref in enumerate(ins):
        place = place_of(i)
        first = pl.multiple_of((place % 4 * 2 + place // 4) * width, 128)
        for n, out in enumerate(outs):
            out[:, pl.ds(first, width)] = ref[:, n * width : (n + 1) * width].astype(jnp.float32)
        rest_ref[place] = ref[:, count * width :]


def join(parts, place_of, count, width):
    rows, columns = parts[0].shape
    shape = jax.ShapeDtypeStruct((rows, 8 * width), jnp.float32)
    rest = jax.ShapeDtypeStruct((8, rows, columns - count * width), parts[0].dtype)
    return pl.pallas_call(
        functools.partial(join_kernel, count, width, place_of),
        out_shape=[shape] * count + [rest],
        compiler_params=pltpu.CompilerParams(vmem_limit_bytes=32 * 2**20),
        cost_estimate=pl.CostEstimate(
            flops=0, bytes_accessed=48 * rows * columns, transcendentals=0
        ),
    )(*parts)


def swap_eight(blocks, *meanwhile, joined=None):
    x, b = here_x(), lax.axis_index("batch")
    got = []
    for k, j in EIGHT:
        block = lax.dynamic_index_in_dim(blocks, (x ^ j) * 4 + (b ^ k), 0, False)
        got.append(across(block, k, j))

    def place_of(i):
        k, j = EIGHT[i]
        return (here_x() ^ j) * 4 + (lax.axis_index("batch") ^ k)

    got = after(got, *meanwhile)
    return join(got, place_of, *joined) if joined else place(got, place_of)


def gather_eight(block, *meanwhile):
    half = block.shape[0] // 2
    over_y = across_batch(block, 2)
    over_x = flip_x(block)
    over_y, over_x = after((over_y, over_x), *meanwhile)
    both_a = flip_x(over_y[:half])
    both_b = across_batch(over_x[half:], 2)
    here = [block, over_x, over_y, both_a, both_b]
    return here + [across_batch(part, 1) for part in here], over_y, (both_a, both_b)


def scatter_first(theirs):
    return [across_batch(theirs[k], 1) for k in range(4)]


def scatter_diagonal(mine, got):
    both = wide(mine[3]) + wide(got[3])
    half = both.shape[0] // 2
    return flip_x(low(both[:half])), across_batch(low(both[half:]), 2)


def scatter_last(mine, got, ways):
    mine, got = after((mine, got), ways)
    over_x, over_y = wide(mine[1]) + wide(got[1]), wide(mine[2]) + wide(got[2])
    half = over_x.shape[0] // 2
    over_y = jnp.concatenate([over_y[:half] + wide(ways[0]), over_y[half:]], axis=0)
    over_x = jnp.concatenate([over_x[:half], over_x[half:] + wide(ways[1])], axis=0)
    return across_batch(low(over_y), 2), flip_x(low(over_x))


def scatter_sum(mine, got, last):
    mine, got = after((mine[0], got[0]), last)
    return wide(mine) + wide(got) + wide(last[0]) + wide(last[1])


def gather_z(block):
    return lax.all_gather(block, "z", axis=0, tiled=True)


def scatter_z(term):
    return lax.psum_scatter(term, "z", scatter_dimension=0, tiled=True)


def cut_kernel(width, full, extra, *refs):
    out_ref = refs[-1]
    ins = refs[:-1]
    rows = out_ref.shape[1]
    for i in range(out_ref.shape[0]):
        first = (i % 4 * 2 + i // 4) * width
        pieces = []
        for n, ref in enumerate(ins[: len(ins) - extra]):
            piece = ref[:, first : first + width]
            if full > width:
                tail = jnp.zeros((rows, full - width), piece.dtype)
                if extra and n == len(ins) - extra - 1:
                    tail = ins[-1][:, : full - width]
                piece = jnp.concatenate([piece, tail], axis=1)
            pieces.append(piece)
        out_ref[i] = jnp.concatenate(pieces, axis=1)


def cut(weights, full, common=None):
    rows = weights[0].shape[0]
    ins = list(weights) + ([] if common is None else [common])
    return pl.pallas_call(
        functools.partial(cut_kernel, weights[0].shape[1] // 8, full, 0 if common is None else 1),
        out_shape=jax.ShapeDtypeStruct((8, rows, full * len(weights)), weights[0].dtype),
        compiler_params=pltpu.CompilerParams(vmem_limit_bytes=32 * 2**20),
        cost_estimate=pl.CostEstimate(
            flops=0, bytes_accessed=4 * weights[0].size * len(weights), transcendentals=0
        ),
    )(*ins)


def whole_rows(parts, first, last):
    return wide(
        jnp.concatenate([parts[i * 4 + j, :, first:last] for j in range(4) for i in range(2)], axis=1)
    )


def in_run_order(own, other, reverse):
    first, second = in_x_order(own, other)
    return (second, first) if reverse else (first, second)


def carried_in(decay, state, reverse):
    z = lax.axis_index("z")
    count = lax.axis_size("z")
    decay_one, decay_two = in_run_order(decay[:, 0], decay[:, 1], reverse)
    state_one, state_two = in_run_order(state[:, 0], state[:, 1], reverse)
    total_a, total_b = decay_one * decay_two, decay_two * state_one + state_two
    enter_a, enter_b = jnp.ones_like(total_a), jnp.zeros_like(total_b)
    bit = 1
    while bit < count:
        got = flip_z(jnp.stack([total_a, total_b]), bit)
        got_a, got_b = got[0], got[1]
        theirs_first = ((z & bit) == 0) if reverse else ((z & bit) != 0)
        enter_b = jnp.where(theirs_first, enter_a * got_b + enter_b, enter_b)
        enter_a = jnp.where(theirs_first, enter_a * got_a, enter_a)
        total_b = jnp.where(theirs_first, total_a * got_b + total_b, got_a * total_b + got_b)
        total_a = total_a * got_a
        bit *= 2
    second = decay_one * enter_b + state_one
    return jnp.stack(in_run_order(enter_b, second, reverse), axis=1)


def scan_kernel(reverse, a_ref, b_ref, cum_ref, out_ref):
    groups, rows, lanes = a_ref.shape
    tiles = rows // 8
    row = lax.broadcasted_iota(jnp.int32, (8, lanes), 0)

    def step(i, carry):
        tile = tiles - 1 - i if reverse else i
        at = pl.ds(pl.multiple_of(tile * 8, 8), 8)
        after = []
        for g in range(groups):
            a, b = a_ref[g, at, :], b_ref[g, at, :]
            for shift in (1, 2, 4):
                by = 8 - shift if reverse else shift
                ok = row < 8 - shift if reverse else row >= shift
                a_far = jnp.where(ok, pltpu.roll(a, by, 0), 1.0)
                b_far = jnp.where(ok, pltpu.roll(b, by, 0), 0.0)
                b = b + a * b_far
                a = a * a_far
            cum, state = carry[g]
            b = b + a * state
            a = a * cum
            cum_ref[g, at, :] = a
            out_ref[g, at, :] = b
            last = 0 if reverse else 7
            after.append(
                (
                    jnp.broadcast_to(a[last : last + 1], (8, lanes)),
                    jnp.broadcast_to(b[last : last + 1], (8, lanes)),
                )
            )
        return tuple(after)

    start = tuple(
        (jnp.ones((8, lanes), jnp.float32), jnp.zeros((8, lanes), jnp.float32))
        for _ in range(groups)
    )
    lax.fori_loop(0, tiles, step, start)


def local_scan(decay, drive, reverse):
    groups, rows, width = decay.shape
    lanes = 128 if width % 128 == 0 else width
    spec = pl.BlockSpec((groups, rows, lanes), lambda i: (0, 0, i))
    shape = jax.ShapeDtypeStruct(decay.shape, jnp.float32)
    return pl.pallas_call(
        functools.partial(scan_kernel, reverse),
        grid=(width // lanes,),
        in_specs=[spec, spec],
        out_specs=[spec, spec],
        out_shape=[shape, shape],
        cost_estimate=pl.CostEstimate(
            flops=20 * decay.size, bytes_accessed=16 * decay.size, transcendentals=0
        ),
    )(decay, drive)


def mlp_kernel(normed_ref, grad_ref, two_ref, down_ref, act_ref, out_ref):
    width = act_ref.shape[1]
    lane = 256 if width % 256 == 0 else width
    normed, grad = normed_ref[...], grad_ref[...]
    for first in range(0, width, lane):
        at, up_at = slice(first, first + lane), slice(width + first, width + first + lane)
        gate = plain_dot(normed, two_ref[:, at])
        up = plain_dot(normed, two_ref[:, up_at])
        act_grad = plain_dot(grad, down_ref[:, at])
        square = gate * gate
        slope = 0.7978845608028654
        bent = jnp.tanh(slope * gate * (1.0 + 0.044715 * square))
        half = 0.5 + 0.5 * bent
        act = half * gate
        act_slope = half + 0.5 * gate * (1.0 - bent * bent) * (slope * (1.0 + 0.134145 * square))
        act_ref[:, at] = low(act * up)
        out_ref[:, at] = low(act_grad * up * act_slope)
        out_ref[:, up_at] = low(act_grad * act)


def mlp(normed, grad, two_full, down_full, rows):
    count, model = normed.shape
    width = down_full.shape[1]

    def block(columns):
        return pl.BlockSpec((rows, columns), lambda i: (i, 0))

    def whole(columns):
        return pl.BlockSpec((model, columns), lambda i: (0, 0))

    return pl.pallas_call(
        mlp_kernel,
        grid=(count // rows,),
        in_specs=[block(model), block(model), whole(2 * width), whole(width)],
        out_specs=[block(width), block(2 * width)],
        out_shape=[
            jax.ShapeDtypeStruct((count, width), jnp.bfloat16),
            jax.ShapeDtypeStruct((count, 2 * width), jnp.bfloat16),
        ],
        compiler_params=pltpu.CompilerParams(vmem_limit_bytes=56 * 2**20),
        cost_estimate=pl.CostEstimate(
            flops=6 * count * model * width,
            bytes_accessed=2 * (2 * count * model + 3 * model * width + 4 * count * width),
            transcendentals=count * width,
        ),
    )(normed, grad, two_full, down_full)


def doc_layout(lengths, first_pos, span_count):
    second = lengths[:, 0:1]
    third = second + lengths[:, 1:2]
    places = first_pos + lax.broadcasted_iota(jnp.int32, (lengths.shape[0], span_count), 1)
    begins = jnp.where(places >= third, third, jnp.where(places >= second, second, 0))
    return places, places == begins, begins


def lru_gates(rate_in, entry_in, conv_in, decay_in, keep_mask, start_mask):
    rate_sig = jax.nn.sigmoid(rate_in)
    entry_sig = jax.nn.sigmoid(entry_in)
    log_decay = -8.0 * rate_sig * jax.nn.softplus(-decay_in)
    drive_scale = jnp.where(start_mask, 1.0, jnp.sqrt(-jnp.expm1(2.0 * log_decay)))
    return (jnp.exp(log_decay) * keep_mask, drive_scale * entry_sig * conv_in)


def inv_root(values):
    return lax.rsqrt(jnp.mean(values * values, axis=-1, keepdims=True) + 1e-06)


def norm_backward(values, scale, gain_vec, incoming):
    weighted = incoming * gain_vec
    inner_mean = jnp.mean(weighted * values, axis=-1, keepdims=True)
    return (
        scale * weighted - values * scale * scale * scale * inner_mean,
        jnp.sum(incoming * values * scale, axis=0),
    )


def head_diagonal(blocks, heads, width):
    size = blocks.shape[0]
    own = lax.broadcasted_iota(jnp.int32, (size, size), 0) // width
    at = lax.broadcasted_iota(jnp.int32, (size, size), 1) // width
    copies = jnp.tile(blocks, (1, heads))
    copies = jnp.pad(copies, ((0, 0), (0, size - heads * width)))
    return jnp.where(own == at, copies, jnp.zeros((), blocks.dtype))


def head_blocks(dense, width):
    size = dense.shape[0]
    own = lax.broadcasted_iota(jnp.int32, (size, size), 0) // width
    at = lax.broadcasted_iota(jnp.int32, (size, size), 1) // width
    pick = lax.broadcasted_iota(jnp.int32, (size, width), 0) % width
    pick = pick == lax.broadcasted_iota(jnp.int32, (size, width), 1)
    return plain_dot(low(jnp.where(own == at, dense, 0.0)), pick.astype(jnp.bfloat16))


def reorder_kernel(chunks, in_ref, out_ref):
    width = in_ref.shape[1] // len(chunks)
    for first in range(0, len(chunks), 2):
        pair = [in_ref[:, c * width : (c + 1) * width] for c in chunks[first : first + 2]]
        out_ref[:, first * width : (first + 2) * width] = jnp.concatenate(pair, axis=1)


def reorder(values, seq, back=False):
    outer = (seq, 4) if back else (4, seq)
    width = values.shape[1] // (4 * seq)
    if width == 64:
        chunks = [j * outer[1] + i for i in range(outer[1]) for j in range(outer[0])]
        return pl.pallas_call(
            functools.partial(reorder_kernel, chunks),
            out_shape=jax.ShapeDtypeStruct(values.shape, values.dtype),
            compiler_params=pltpu.CompilerParams(vmem_limit_bytes=32 * 2**20),
            cost_estimate=pl.CostEstimate(
                flops=0, bytes_accessed=8 * values.size, transcendentals=0
            ),
        )(values)
    cut = values.reshape(values.shape[0], *outer, width)
    return cut.transpose(0, 2, 1, 3).reshape(values.shape)


def shards(
    tokens,
    doc_lengths,
    out_grad,
    mix_gain,
    branch_weight,
    input_weight,
    branch_bias,
    input_bias,
    conv_taps,
    conv_bias,
    rate_weight,
    entry_weight,
    rate_bias,
    entry_bias,
    decay_param,
    out_weight,
    out_bias,
    mlp_gain,
    gate_weight,
    up_weight,
    down_weight,
):
    z_count = lax.axis_size("z")
    seq = 2 * z_count
    s = 2 * lax.axis_index("z") + here_x()
    rows, model = tokens.shape[1:]
    block_w = rate_weight.shape[1]
    tap_count = conv_taps.shape[1]
    width = branch_weight.shape[1] // 8
    full_w = -(-width // 128) * 128
    hidden_w = gate_weight.shape[1] // 8
    heads = width // block_w
    own_r = conv_bias.shape[0]
    own_d = mix_gain.shape[0]
    groups, blocks = 4, 8
    every = blocks * rows

    pack_w = -(-(2 * block_w + tap_count + 6) // 128) * 128
    lengths = jnp.concatenate([doc_lengths] + [across_batch(doc_lengths, k) for k in (2, 1, 3)], 0)
    model_vec = jnp.stack([mix_gain, mlp_gain, out_bias], axis=1)
    model_vec = jnp.pad(model_vec, ((0, 0), (0, 125)))
    rec_cut = cut([branch_weight, out_weight, input_weight], full_w, model_vec)
    weight_rows = 8 * own_d
    rec_rows = swap_eight(rec_cut).reshape(weight_rows, -1)

    own_tokens = reorder(after(tokens[0], rec_cut), seq)
    vectors = jnp.stack(
        [branch_bias, input_bias, conv_bias, rate_bias, entry_bias, decay_param], axis=1
    )
    pack = jnp.concatenate([after(rate_weight, rec_cut), entry_weight, conv_taps, vectors], axis=1)
    pack = jnp.pad(pack, ((0, 0), (0, pack_w - pack.shape[1])))
    pack = jnp.concatenate(in_x_order(pack, flip_x(pack)), axis=0)
    first = gather_z(jnp.concatenate([rec_rows[:, 2 * full_w :], pack], axis=0)).reshape(z_count, -1, pack_w)
    tokens_parts, _, tokens_last = gather_eight(after(own_tokens, rec_rows, lengths))

    input_all = first[:, :weight_rows].reshape(model, full_w)
    pack_all = first[:, weight_rows:].reshape(-1, pack_w)
    model_full = wide(input_all[:, width : width + 3]).T
    mix_scale, mlp_scale, out_b = model_full[0], model_full[1], model_full[2]
    rec_full = gather_z(rec_rows[:, : 2 * full_w])
    branch_full, out_full = rec_full[:, :full_w], rec_full[:, full_w:]

    mlp_cut = cut(after((gate_weight, up_weight, down_weight), rec_rows), hidden_w)
    mlp_sent = after(mlp_cut, tokens_last)
    grad_low = reorder(after(out_grad[0], rec_rows), seq)

    by_channel = lax.dynamic_slice_in_dim(pack_all, here_x() * width, width, 0)
    by_channel = jnp.pad(by_channel, ((0, full_w - width), (0, 0)))
    rate_dense = head_diagonal(by_channel[:, :block_w], heads, block_w)
    entry_dense = head_diagonal(by_channel[:, block_w : 2 * block_w], heads, block_w)
    channel_vec = wide(by_channel[:, 2 * block_w : 2 * block_w + tap_count + 6]).T
    tap_vals = channel_vec[:tap_count]
    branch_b, input_b, conv_b, rate_b, entry_b, decay_full = [
        channel_vec[tap_count + i] for i in range(6)
    ]
    layouts = [doc_layout(lengths, place * rows, rows + tap_count - 1) for place in (s, s ^ 1)]
    places, start_mask, begins = [
        jnp.stack([one, other], axis=1).reshape(blocks, -1) for one, other in zip(*layouts)
    ]
    own_start = start_mask[:, :rows, None]
    keep_mask = 1.0 - own_start.astype(jnp.float32)

    normed_low = [low(wide(part) * inv_root(wide(part)) * mix_scale) for part in tokens_parts]
    normed_low = lax.optimization_barrier(jnp.concatenate(normed_low, axis=0))
    own_channel = jnp.arange(full_w) < width
    input_full = jnp.where(own_channel, input_all, jnp.zeros((), jnp.bfloat16))
    conv_in = low(plain_dot(normed_low, input_full) + input_b).reshape(groups, 2, rows, full_w)
    mlp_rows = swap_eight(mlp_sent, conv_in).reshape(weight_rows, -1)
    gate_full = gather_z(mlp_rows[:, :hidden_w])
    up_full = gather_z(mlp_rows[:, hidden_w : 2 * hidden_w])
    down_full = gather_z(mlp_rows[:, 2 * hidden_w :])
    two_full = jnp.concatenate([gate_full, up_full], axis=1)
    x = here_x()

    def rims(values, first, last, hops):
        edge = values[:, :, first:last]
        forward = hops[0][1] > hops[0][0]
        sent_block, near_block = in_x_order(edge[:, 0], edge[:, 1])
        if forward:
            sent_block, near_block = near_block, sent_block
        got = along_z(sent_block, hops)
        at_edge = x == 0 if forward else x == 1
        own_rim = jnp.where(at_edge, got, edge[:, 1])
        other_rim = jnp.where(at_edge, edge[:, 0], got)
        return jnp.stack([own_rim, other_rim], axis=1)

    before = rims(conv_in, rows - RIM, rows, [(i, i + 1) for i in range(z_count - 1)])
    conv_in = jnp.concatenate([before, conv_in], axis=2).reshape(blocks, RIM + rows, full_w)

    def behind(offset):
        return conv_in[:, RIM - offset : RIM - offset + rows]

    def valid(offset, ahead):
        at = slice(offset, offset + rows) if ahead else slice(0, rows)
        return wide(places[:, at] - offset >= begins[:, at])[:, :, None]

    conv_val = jnp.zeros((blocks, rows, full_w), jnp.float32) + conv_b
    for offset in range(tap_count):
        conv_val = conv_val + tap_vals[offset] * wide(behind(offset)) * valid(offset, False)
    conv_low = low(conv_val)
    conv_flat = after(conv_low, rec_full).reshape(every, full_w)
    rate_pre = (plain_dot(conv_flat, rate_dense) + rate_b).reshape(blocks, rows, full_w)
    entry_pre = (plain_dot(conv_flat, entry_dense) + entry_b).reshape(blocks, rows, full_w)

    def gate_piece(rate_in, entry_in, conv_part, decay_in):
        return lru_gates(rate_in, entry_in, conv_part, decay_in, keep_mask, own_start)

    (decay_a, drive), gate_pull = jax.vjp(gate_piece, rate_pre, entry_pre, wide(conv_low), decay_full)
    cum_decay, local_state = local_scan(after(decay_a, mlp_rows), drive, False)
    grad_parts, _, grad_last = gather_eight(after(grad_low, mlp_rows), cum_decay)
    grad_all = jnp.concatenate(grad_parts, axis=0)
    carry_in = carried_in(
        cum_decay[:, -1].reshape(groups, 2, full_w), local_state[:, -1].reshape(groups, 2, full_w), False
    ).reshape(blocks, full_w)
    hidden = local_state + cum_decay * carry_in[:, None]
    branch_pre = plain_dot(normed_low, branch_full) + branch_b
    branch_val, branch_pull = jax.vjp(gelu_tanh, branch_pre)
    merged = after(low(hidden.reshape(every, full_w) * branch_val), gate_full, grad_last)

    def token_terms(part, weight):
        return low(against_rows(part, weight)).reshape(4, rows, model)

    def eight_terms(values, weight):
        theirs = token_terms(values[every // 2 :], weight)
        return token_terms(values[: every // 2], weight), theirs

    inputs = wide(own_tokens)
    mine, theirs = eight_terms(merged, out_full)
    got = scatter_first(theirs)
    ways = after(scatter_diagonal(mine, got), grad_parts)
    last = after(scatter_last(mine, got, ways), up_full, grad_all)
    residual = inputs + scatter_sum(mine, got, last) + out_b
    scale_two = inv_root(residual)
    normed_two = low(residual * scale_two * mlp_scale)
    normed_two_all = jnp.concatenate(gather_eight(normed_two)[0], axis=0)

    activated, two_grad = mlp(after(normed_two_all, down_full), grad_all, two_full, down_full, rows)
    theirs = token_terms(two_grad[every // 2 :], two_full)
    got = scatter_first(theirs)
    mine = token_terms(two_grad[: every // 2], two_full)
    down_term = low(outer_sum(grad_all, activated))
    ways = after(scatter_diagonal(mine, got), down_term)
    last = scatter_last(mine, got, ways)
    two_term = low(outer_sum(normed_two_all, two_grad))
    down_share = scatter_z(down_term)
    two_share = scatter_z(two_term)
    last = after(last, two_term)
    normed_two_grad = scatter_sum(mine, got, last)
    residual_part, mlp_gain_term = norm_backward(residual, scale_two, mlp_scale, normed_two_grad)
    residual_grad = wide(grad_low) + residual_part
    mix_low = low(residual_grad)
    out_bias_term = jnp.sum(wide(mix_low), axis=0)
    block_mine, block_theirs = eight_terms(activated, down_full)
    mix_all = jnp.concatenate(gather_eight(mix_low, block_mine, block_theirs)[0], axis=0)

    merged_grad = plain_dot(after(mix_all, down_share), out_full)
    state_grad = (merged_grad * branch_val).reshape(blocks, rows, full_w)
    next_decay = jnp.concatenate([decay_a[:, 1:], jnp.ones((blocks, 1, full_w), jnp.float32)], axis=1)
    cum_back, local_adjoint = local_scan(next_decay, state_grad, True)
    first_decay = decay_a[:, 0]
    adjoint_in = carried_in(
        (first_decay * cum_back[:, 0]).reshape(groups, 2, full_w),
        (first_decay * local_adjoint[:, 0]).reshape(groups, 2, full_w),
        True,
    ).reshape(blocks, full_w)
    branch_low = low(branch_pull(merged_grad * hidden.reshape(every, full_w))[0])
    out_term = low(outer_sum(mix_all, merged))
    branch_term = outer_sum(normed_low, branch_low)
    rec_term = jnp.concatenate([out_term, low(branch_term)], axis=1)
    rec_share = scatter_z(rec_term)
    adjoint = local_adjoint + cum_back * after(adjoint_in, rec_term)[:, None]
    prev_state = jnp.concatenate([carry_in[:, None], hidden[:, :-1]], axis=1)
    rate_grad, entry_grad, conv_direct, decay_term = gate_pull((adjoint * prev_state, adjoint))
    rate_low = low(rate_grad).reshape(every, full_w)
    entry_low = low(entry_grad).reshape(every, full_w)
    conv_grad = (
        conv_direct.reshape(every, full_w)
        + against_rows(rate_low, rate_dense)
        + against_rows(entry_low, entry_dense)
    )
    conv_grad_low = low(conv_grad).reshape(groups, 2, rows, full_w)
    after_rim = rims(conv_grad_low, 0, RIM, [(i + 1, i) for i in range(z_count - 1)])
    grad_ext = wide(jnp.concatenate([conv_grad_low, after_rim[:, :, : tap_count - 1]], axis=2))
    grad_ext = grad_ext.reshape(blocks, rows + tap_count - 1, full_w)
    conv_grad_f = wide(conv_grad_low).reshape(blocks, rows, full_w)
    input_grad = jnp.zeros((blocks, rows, full_w), jnp.float32)
    for offset in range(tap_count):
        input_grad = (
            input_grad
            + tap_vals[offset] * grad_ext[:, offset : offset + rows] * valid(offset, True)
        )
    input_low = low(input_grad).reshape(every, full_w)
    both_low = jnp.concatenate([branch_low, input_low], axis=1)
    both_full = jnp.concatenate([branch_full, input_full], axis=1)
    mix_theirs = token_terms(both_low[every // 2 :], both_full)
    mix_mine = token_terms(both_low[: every // 2], both_full)
    got = scatter_first(mix_theirs)
    ways = scatter_diagonal(mix_mine, got)

    input_low, branch_sum = after((input_low, branch_low), mix_mine, mix_theirs)
    input_term = outer_sum(normed_low, input_low)
    conv_grad_f, rate_low, entry_low = after((conv_grad_f, rate_low, entry_low), mix_mine, mix_theirs)
    tap_terms = [
        jnp.sum(conv_grad_f * valid(offset, False) * wide(behind(offset)), axis=(0, 1))
        for offset in range(tap_count)
    ]
    mix_gain_term = branch_term * wide(branch_full) + input_term * wide(input_full)
    mix_gain_term = jnp.sum(mix_gain_term, axis=1) / mix_scale
    model_terms = jnp.stack([mix_gain_term, mlp_gain_term, out_bias_term], axis=1)
    model_terms = jnp.pad(model_terms, ((0, 0), (0, full_w - width - 3)))
    input_block = low(jnp.concatenate([input_term[:, :width], model_terms], axis=1))

    rate_term = head_blocks(outer_sum(conv_flat, rate_low), block_w)
    entry_term = head_blocks(outer_sum(conv_flat, entry_low), block_w)

    def column_sum(values):
        return jnp.sum(wide(values), axis=0)

    channel_terms = jnp.stack(
        tap_terms
        + [
            column_sum(branch_sum),
            column_sum(input_low),
            jnp.sum(conv_grad_f, axis=(0, 1)),
            column_sum(rate_low),
            column_sum(entry_low),
            decay_term,
        ],
        axis=1,
    )
    small = low(jnp.concatenate([rate_term, entry_term, channel_terms], axis=1))[:width]
    small = jnp.pad(small, ((0, 0), (0, pack_w - small.shape[1])))
    small = lax.dynamic_update_slice_in_dim(
        jnp.zeros((2 * width, pack_w), jnp.bfloat16), small, x * width, 0
    )
    input_block = jnp.concatenate(
        [input_block.reshape(z_count, weight_rows, -1), small.reshape(z_count, 2 * own_r, -1)], axis=1
    ).reshape(-1, pack_w)
    input_share = scatter_z(after(input_block, rec_share))
    ways = after(ways, two_share)
    block_got = scatter_first(block_theirs)
    block_ways = scatter_diagonal(block_mine, after(block_got, ways))
    last = after(scatter_last(mix_mine, got, ways), input_block)
    normed_grad = scatter_sum(mix_mine, got, last)
    block_last = scatter_last(block_mine, block_got, after(block_ways, last))
    input_part, _ = norm_backward(inputs, inv_root(inputs), mix_scale, normed_grad)
    tokens_grad = reorder(residual_grad + input_part, seq, True)[None]
    shares = [two_share, down_share, rec_share, input_share[:weight_rows]]
    shares = jnp.concatenate(shares, axis=1).reshape(8, own_d, -1)
    block_last = after(block_last, shares)
    block_out = reorder(low(residual + scatter_sum(block_mine, block_got, block_last)), seq, True)
    *mlp_grads, rec_back = swap_eight(shares, normed_grad, joined=(3, hidden_w))
    small_share = after(input_share[weight_rows:], normed_grad).reshape(2, own_r, pack_w)
    channel_sum = wide(lax.dynamic_index_in_dim(small_share, x, 0, False)) + wide(
        flip_x(lax.dynamic_index_in_dim(small_share, 1 - x, 0, False))
    )
    vec_sum = channel_sum[:, 2 * block_w :]
    model_at = 2 * full_w + width
    model_out = jnp.sum(wide(rec_back[:, :, model_at : model_at + 3]), axis=0)
    at = tap_count
    return (
        block_out[None],
        tokens_grad,
        model_out[:, 0],
        whole_rows(rec_back, full_w, full_w + width),
        whole_rows(rec_back, 2 * full_w, 2 * full_w + width),
        vec_sum[:, at],
        vec_sum[:, at + 1],
        vec_sum[:, :tap_count],
        vec_sum[:, at + 2],
        channel_sum[:, :block_w],
        channel_sum[:, block_w : 2 * block_w],
        vec_sum[:, at + 3],
        vec_sum[:, at + 4],
        vec_sum[:, at + 5],
        whole_rows(rec_back, 0, width),
        model_out[:, 2],
        model_out[:, 1],
        *mlp_grads,
    )


def solution(mesh):
    batch, seq = mesh.shape["batch"], mesh.shape["seq"]
    fine = Mesh(mesh.devices.reshape(batch, seq // 2, 2), ("batch", "z", "x"))
    everywhere = ("batch", "z", "x")
    vector, matrix = P(everywhere), P(everywhere, None)
    block = P("batch", ("z", "x"), None)
    weights = (
        vector,
        matrix,
        matrix,
        vector,
        vector,
        matrix,
        vector,
        matrix,
        matrix,
        vector,
        vector,
        vector,
        matrix,
        vector,
        vector,
        matrix,
        matrix,
        matrix,
    )
    return jax.shard_map(
        shards,
        mesh=fine,
        in_specs=(block, P("batch", None), block) + weights,
        out_specs=(block, block) + weights,
        check_vma=False,
    )
```
